128 devices in a mesh: stream: 16 (over y_lo, z, core), span: 8 (over x, y_hi).
Axes of the slice: x: 4, y: 4 (y_hi: 2, y_lo: 2; y = y_hi * 2 + y_lo), z: 4, core: 2. Of those that a mesh axis runs over, the one named last changes fastest.
Arguments:
- conserved: float32 [5, 32, 256, 512], P(None, 'stream', 'span'), may hold values from -1.1 to 7, as said below
- phase_mask: int32 [32, 256, 512], P('stream', 'span'), may hold values from 0 to 2, as said below
- diag_inverse: float32 [5, 5, 32, 256, 512], P(None, None, 'stream', 'span'), may hold values from -0.25 to 2.9
Outputs:
- update: float32 [5, 32, 256, 512], P(None, 'stream', 'span')
- residual: float32 [5, 32, 256, 512], P(None, 'stream', 'span')
The draws below stay inside these ranges and needn't reach their ends.
Inputs may be any that keep to these rules, and one draw needn't show every extreme that they name: `phase_mask`: phase region of each cell: 0 liquid, 1 vapor, 2 mixture. `conserved`: each cell holds a stiffened gas of its phase at a pressure of 0.8 to 1.2, every velocity component within 0.15 of zero and a sound speed of 0.7 or more.
All inputs are finite; a program needn't handle non-finite values.
Results may differ from the reference program's by a relative error of at most 0.0003.
Values sent between devices are 32-bit elements; how exact they have to be, the bound alone decides.
A program may use at most 192 MiB of HBM per device.

```python
import jax
import jax.numpy as jnp
from jax import lax

NORMAL_CELLS = 512
STREAM_PLANES = 32
SPAN_CELLS = 256


def heat_tables(phase_mask):
    heat_ratio = jnp.where(phase_mask == 0, 4.4, jnp.where(phase_mask == 1, 1.4, 2.0)).astype(jnp.float32)
    stiffness = jnp.where(phase_mask == 0, 1.0, jnp.where(phase_mask == 1, 0.0, 0.5)).astype(jnp.float32)
    return (heat_ratio, stiffness)


def common_fields(key):
    grid = (STREAM_PLANES, SPAN_CELLS, NORMAL_CELLS)
    phase_mask = jax.random.randint(jax.random.fold_in(key, 11), grid, 0, 3).astype(jnp.int32)
    heat_ratio, stiffness = heat_tables(phase_mask)
    sound_low = jnp.where(phase_mask == 0, 1.2, jnp.where(phase_mask == 1, 0.8, 0.7)).astype(jnp.float32)
    sound_high = jnp.where(phase_mask == 0, 1.6, jnp.where(phase_mask == 1, 1.0, 0.9)).astype(jnp.float32)
    draws = [jax.random.uniform(jax.random.fold_in(key, 12 + number), grid, jnp.float32) for number in range(6)]
    pressure = 0.8 + 0.4 * draws[0]
    acoustic_celerity = sound_low + (sound_high - sound_low) * draws[1]
    speed_flow = 0.3 * draws[2] - 0.15
    speed_span = 0.3 * draws[3] - 0.15
    speed_wall = 0.3 * draws[4] - 0.15
    density = heat_ratio * (pressure + stiffness) / (acoustic_celerity * acoustic_celerity)
    kinetic = 0.5 * density * (speed_flow * speed_flow + speed_span * speed_span + speed_wall * speed_wall)
    energy = (pressure + heat_ratio * stiffness) / (heat_ratio - 1.0) + kinetic
    conserved = jnp.stack([density, density * speed_flow, density * speed_span, density * speed_wall, energy])
    radius = jnp.abs(speed_flow) + acoustic_celerity
    return (phase_mask, conserved, radius)


def draw_conserved(key, part):
    return common_fields(key)[1].astype(jnp.float32)


def draw_phase_mask(key, part):
    return common_fields(key)[0]


def draw_diag_inverse(key, part):
    radius = common_fields(key)[2]
    upwind = jnp.concatenate([radius[:1], radius[:-1]], axis=0)
    downwind = jnp.concatenate([radius[1:], radius[-1:]], axis=0)
    scaling = 1.0 / (0.5 * jnp.sqrt(upwind * downwind))
    slow_share = 0.5
    is_slow = jax.random.uniform(jax.random.fold_in(key, 21), (5, SPAN_CELLS, NORMAL_CELLS), jnp.float32) < slow_share
    lasting = jax.random.uniform(jax.random.fold_in(key, 22), (5, SPAN_CELLS, NORMAL_CELLS), jnp.float32, 0.3, 1.0)
    damped_wave_rate = jnp.exp(jnp.log(0.3) * lasting / STREAM_PLANES)[:, None]
    jitter = jax.random.uniform(jax.random.fold_in(key, 23), (5, STREAM_PLANES, SPAN_CELLS, NORMAL_CELLS), jnp.float32)
    damped_wave_rate = damped_wave_rate * (1.0 - 0.2 * jitter / STREAM_PLANES)
    cavity_plane_index = jax.random.uniform(jax.random.fold_in(key, 24), (STREAM_PLANES,), jnp.float32) < 2.0 / STREAM_PLANES
    cavity_threshold = jax.random.uniform(jax.random.fold_in(key, 25), (5, STREAM_PLANES, SPAN_CELLS, NORMAL_CELLS), jnp.float32, 0.5, 0.8)
    damped_wave_rate = jnp.where(cavity_plane_index[None, :, None, None], damped_wave_rate * cavity_threshold, damped_wave_rate)
    fast_rate = jax.random.uniform(jax.random.fold_in(key, 26), (5, STREAM_PLANES, SPAN_CELLS, NORMAL_CELLS), jnp.float32, 0.2, 0.6)
    diagonal = jnp.where(is_slow[:, None], damped_wave_rate, fast_rate) * scaling[None]
    couple = jax.random.uniform(jax.random.fold_in(key, 27), (5, 5, STREAM_PLANES, SPAN_CELLS, NORMAL_CELLS), jnp.float32, -0.08, 0.08) * scaling[None, None]
    couple = jnp.where(is_slow[:, None, None], 0.0, couple)
    unit = jnp.eye(5, dtype=jnp.float32)[:, :, None, None, None]
    return (unit * diagonal[:, None] + (1.0 - unit) * couple).astype(jnp.float32)


def setup_inputs(seed: int = 0) -> dict:
    streams_of = jax.random.split(jax.random.key(seed), 4)
    return {
        "conserved": draw_conserved(jax.random.fold_in(streams_of[3], 71), 0),
        "phase_mask": draw_phase_mask(jax.random.fold_in(streams_of[3], 71), 0),
        "diag_inverse": draw_diag_inverse(jax.random.fold_in(streams_of[3], 71), 0),
    }


face_area = 0.0625

def eos_table(phase_mask):
    heat_ratio = jnp.where(phase_mask == 0, 4.4, jnp.where(phase_mask == 1, 1.4, 2.0)).astype(jnp.float32)
    stiffness = jnp.where(phase_mask == 0, 1.0, jnp.where(phase_mask == 1, 0.0, 0.5)).astype(jnp.float32)
    return (heat_ratio, stiffness)

def derive(conserved, phase_mask):
    heat_ratio, stiffness = eos_table(phase_mask)
    density = conserved[0]
    speed_flow = conserved[1] / density
    speed_span = conserved[2] / density
    speed_wall = conserved[3] / density
    kinetic = 0.5 * density * (speed_flow * speed_flow + speed_span * speed_span + speed_wall * speed_wall)
    pressure = (heat_ratio - 1.0) * (conserved[4] - kinetic) - heat_ratio * stiffness
    acoustic_celerity = jnp.sqrt(heat_ratio * (pressure + stiffness) / density)
    return jnp.concatenate([conserved, pressure[None], acoustic_celerity[None]], axis=0)

def physical(fields, normal, speed):
    pressure = fields[5]
    pieces = [fields[normal]]
    for column in (1, 2, 3):
        adding = fields[column] * speed
        if column == normal:
            adding = adding + pressure
        pieces.append(adding)
    pieces.append((fields[4] + pressure) * speed)
    return pieces

def star_flux(fields, normal, speed, wave, moving, contact, fluxes):
    factor = moving / (wave - contact)
    starred = [factor]
    for column in (1, 2, 3):
        if column == normal:
            starred.append(factor * contact)
        else:
            starred.append(factor * (fields[column] / fields[0]))
    starred.append(factor * (fields[4] / fields[0] + (contact - speed) * (contact + fields[5] / moving)))
    return [fluxes[column] + wave * (starred[column] - fields[column]) for column in range(5)]

def riemann_flux(left_state, right_state, normal):
    speed_left = left_state[normal] / left_state[0]
    speed_right = right_state[normal] / right_state[0]
    wave_left = jnp.minimum(speed_left - left_state[6], speed_right - right_state[6])
    wave_right = jnp.maximum(speed_left + left_state[6], speed_right + right_state[6])
    mass_left = left_state[0] * (wave_left - speed_left)
    mass_right = right_state[0] * (wave_right - speed_right)
    contact = (right_state[5] - left_state[5] + mass_left * speed_left - mass_right * speed_right) / (mass_left - mass_right)
    flux_left = physical(left_state, normal, speed_left)
    flux_right = physical(right_state, normal, speed_right)
    star_left = star_flux(left_state, normal, speed_left, wave_left, mass_left, contact, flux_left)
    star_right = star_flux(right_state, normal, speed_right, wave_right, mass_right, contact, flux_right)
    chosen = []
    for column in range(5):
        chosen.append(jnp.where(wave_left >= 0.0, flux_left[column], jnp.where(contact >= 0.0, star_left[column], jnp.where(wave_right >= 0.0, star_right[column], flux_right[column]))))
    return jnp.stack(chosen)

def block_residual(padded):
    inside = padded[:, 1:-1, 1:-1]
    flux_along = riemann_flux(padded[:, :-1, 1:-1], padded[:, 1:, 1:-1], 1)
    flux_across = riemann_flux(padded[:, 1:-1, :-1], padded[:, 1:-1, 1:], 2)
    neighbour = jnp.concatenate([inside[:, :, :, 1:], inside[:, :, :, -1:]], axis=3)
    flux_normal = riemann_flux(inside, neighbour, 3)
    surface = inside[:, :, :, :1]
    mirror = jnp.concatenate([surface[:3], -surface[3:4], surface[4:]], axis=0)
    flux_wall = riemann_flux(mirror, surface, 3)
    below = jnp.concatenate([flux_wall, flux_normal[:, :, :, :-1]], axis=3)
    return face_area * (flux_along[:, 1:] - flux_along[:, :-1] + (flux_across[:, :, 1:] - flux_across[:, :, :-1]) + (flux_normal - below))

def apply_block(matrix, vector):
    summed = matrix[:, 0] * vector[0]
    for column in range(1, 5):
        summed = summed + matrix[:, column] * vector[column]
    return summed

def forward(diag_inverse, source, coupling, incoming):
    planes = source.shape[1]

    def advance(plane_at, carried):
        flowing, outputs = carried
        matrix = lax.dynamic_index_in_dim(diag_inverse, plane_at, 2, keepdims=False)
        entry = lax.dynamic_index_in_dim(source, plane_at, 1, keepdims=False)
        result = apply_block(matrix, entry + flowing)
        outputs = lax.dynamic_update_index_in_dim(outputs, result, plane_at, 1)
        weight = lax.dynamic_index_in_dim(coupling, plane_at, 0, keepdims=False)
        return (weight * result, outputs)
    flowing, outputs = lax.fori_loop(0, planes, advance, (incoming, jnp.zeros_like(source)))
    return (outputs, flowing)

def backward(diag_inverse, sweep, coupling, incoming):
    planes = sweep.shape[1]

    def retreat(turn_at, carried):
        flowing, outputs = carried
        plane_at = planes - 1 - turn_at
        matrix = lax.dynamic_index_in_dim(diag_inverse, plane_at, 2, keepdims=False)
        earlier = lax.dynamic_index_in_dim(sweep, plane_at, 1, keepdims=False)
        result = earlier + apply_block(matrix, flowing)
        outputs = lax.dynamic_update_index_in_dim(outputs, result, plane_at, 1)
        weight = lax.dynamic_index_in_dim(coupling, plane_at, 0, keepdims=False)
        return (weight * result, outputs)
    flowing, outputs = lax.fori_loop(0, planes, retreat, (incoming, jnp.zeros_like(sweep)))
    return (outputs, flowing)

def residual_field(conserved, phase_mask):
    fields = derive(conserved, phase_mask)
    coupling = 0.5 * (jnp.abs(fields[1] / fields[0]) + fields[6])
    padded = jnp.concatenate([fields[:, :1], fields, fields[:, -1:]], axis=1)
    padded = jnp.concatenate([padded[:, :, -1:], padded, padded[:, :, :1]], axis=2)

    def one_plane(plane_at):
        return block_residual(lax.dynamic_slice_in_dim(padded, plane_at, 3, 1))[:, 0]
    stacked = lax.map(one_plane, jnp.arange(STREAM_PLANES, dtype=jnp.int32))
    return (jnp.moveaxis(stacked, 0, 1), coupling)

def reference(conserved, phase_mask, diag_inverse):
    residual, coupling = residual_field(conserved, phase_mask)
    source = -residual
    zero_in = jnp.zeros(source[:, 0].shape, jnp.float32)
    sweep = forward(diag_inverse, source, coupling, zero_in)[0]
    update = backward(diag_inverse, sweep, coupling, zero_in)[0]
    return (update, residual)
```

```python
import jax
import jax.numpy as jnp
from jax import lax
from jax.experimental import pallas as pl
from jax.experimental.pallas import tpu as pltpu
from jax.sharding import PartitionSpec as P

face_area = 0.0625
MESH = pl.DeviceIdType.MESH
CHIPS = 8
SOLVER = 1
f32 = jnp.float32


def xor_chip(chip, k):
    return (
        ((k // 4 + chip // 4) % 2) * 4 + ((k // 2 + chip // 2) % 2) * 2 + (k + chip) % 2
    )


def eos(phase):
    ratio = jnp.where(phase == 0, 4.4, jnp.where(phase == 1, 1.4, 2.0)).astype(f32)
    stiff = jnp.where(phase == 0, 1.0, jnp.where(phase == 1, 0.0, 0.5)).astype(f32)
    return ratio, stiff


def primitives(cons, phase):
    ratio, stiff = eos(phase)
    density = cons[0]
    inverse = 1.0 / density
    u1, u2, u3 = cons[1] * inverse, cons[2] * inverse, cons[3] * inverse
    kinetic = 0.5 * density * (u1 * u1 + u2 * u2 + u3 * u3)
    pressure = (ratio - 1.0) * (cons[4] - kinetic) - ratio * stiff
    sound = jnp.sqrt(ratio * (pressure + stiff) * inverse)
    return [density, u1, u2, u3, cons[4] * inverse, pressure, sound]


def hllc(left, right, normal):
    ql, qr = left[normal], right[normal]
    cl, cr = left[6], right[6]
    sl = jnp.minimum(ql - cl, qr - cr)
    sr = jnp.maximum(ql + cl, qr + cr)
    ml = left[0] * (sl - ql)
    mr = right[0] * (sr - qr)
    contact = (right[5] - left[5] + ml * ql - mr * qr) / (ml - mr)
    supersonic = sl >= 0.0
    ahead = contact >= 0.0
    use_left = jnp.logical_or(supersonic, ahead)
    starred = jnp.logical_and(
        jnp.logical_not(supersonic), jnp.logical_or(ahead, sr >= 0.0)
    )
    pick = lambda a, b: jnp.where(use_left, a, b)
    s, m, q = pick(sl, sr), pick(ml, mr), pick(ql, qr)
    p, e = pick(left[5], right[5]), pick(left[4], right[4])
    ss = jnp.where(starred, contact, q)
    inv = 1.0 / (s - ss)
    mass = m * inv * ss
    out = [mass]
    for d in (1, 2, 3):
        if d == normal:
            out.append(s * mass - q * m + p)
        else:
            out.append(pick(left[d], right[d]) * mass)
    out.append(p * q + e * mass + s * (ss - q) * (mass + p * inv))
    return out


def matvec(mat, vec):
    return [
        mat(i, 0) * vec[0]
        + mat(i, 1) * vec[1]
        + mat(i, 2) * vec[2]
        + mat(i, 3) * vec[3]
        + mat(i, 4) * vec[4]
        for i in range(5)
    ]


def kernel(
    cons, phase, diag, upd, resid,
    qp, pp, qg, pg, eq, ep, row_out, row_in, dv, prim, acc, swp, res, upv,
    m_out, n_out, m_all, n_all,
    g_out, g_all, f_out, f_all, h_out, h_all, w_out, w_all,
    loc_sem, chip_send, chip_recv, halo_send, halo_recv, row_send, row_recv,
    m_send, m_recv, n_send, n_recv, g_send, g_recv, f_send, f_recv,
    h_send, h_recv, w_send, w_recv, out_sem, out_send, out_recv,
):
    stream = lax.axis_index("stream")
    span = lax.axis_index("span")
    spans = lax.axis_size("span")
    core = stream % 2
    chip = stream // 2
    other = 1 - core
    span_up = (span + 1) % spans
    span_down = (span + spans - 1) % spans

    def dev(chip_at, core_at, span_at=None):
        return {
            "stream": chip_at * 2 + core_at,
            "span": span if span_at is None else span_at,
        }

    def remote(src, dst, send, recv, device):
        return pltpu.make_async_remote_copy(
            src_ref=src, dst_ref=dst, send_sem=send, recv_sem=recv,
            device_id=device, device_id_type=MESH,
        )

    barrier = pltpu.get_barrier_semaphore()

    def greet(device):
        pl.semaphore_signal(barrier, inc=1, device_id=device, device_id_type=MESH)

    @pl.loop(1, 16)
    def _(step):
        pl.semaphore_signal(
            barrier, inc=1,
            device_id={"stream": (stream + step) % 16, "span": span},
            device_id_type=MESH,
        )

    span_near = core * span_up + other * span_down
    span_far = core * span_down + other * span_up
    greet(dev(chip, core, span_near))
    greet(dev(chip, other, span_near))
    greet(dev(chip, core, span_far))

    mine = pl.ds(2 * core, 2)
    src_rows = pl.ds(pl.multiple_of(8 * core, 8), 24)
    dst_rows = pl.ds(pl.multiple_of(8 * other, 8), 24)
    edge_rows = pl.ds(pl.multiple_of(24 * other, 8), 8)
    half = pl.ds(pl.multiple_of(16 * core, 8), 16)
    other_half = pl.ds(pl.multiple_of(16 * other, 8), 16)
    loads = [
        pltpu.make_async_copy(cons.at[:, :, src_rows], qp.at[:, mine, dst_rows], loc_sem.at[0]),
        pltpu.make_async_copy(phase.at[:, src_rows], pp.at[mine, dst_rows], loc_sem.at[1]),
        pltpu.make_async_copy(cons.at[:, :, edge_rows], eq, loc_sem.at[2]),
        pltpu.make_async_copy(phase.at[:, edge_rows], ep, loc_sem.at[3]),
        pltpu.make_async_copy(diag.at[:, :, :, half], dv.at[:, :, mine], loc_sem.at[4]),
    ]
    for copy in loads:
        copy.start()

    for copy in loads[:4]:
        copy.wait()

    def pack_row(side, cell, phase_cell):
        for ch in range(5):
            for plane in range(2):
                row_out[side, pl.ds(ch * 2 + plane, 1), :] = cell(ch, plane)
        for plane in range(2):
            row_out[side, pl.ds(10 + plane, 1), :] = phase_cell(plane).astype(f32)
        row_out[side, pl.ds(12, 4), :] = jnp.zeros((4, 512), f32)

    @pl.when(core == 0)
    def _():
        pack_row(0, lambda c, p: eq[c, p, pl.ds(7, 1), :], lambda p: ep[p, pl.ds(7, 1), :])
        pack_row(1, lambda c, p: qp[c, p, pl.ds(8, 1), :], lambda p: pp[p, pl.ds(8, 1), :])

    @pl.when(core == 1)
    def _():
        pack_row(0, lambda c, p: qp[c, 2 + p, pl.ds(23, 1), :], lambda p: pp[2 + p, pl.ds(23, 1), :])
        pack_row(1, lambda c, p: eq[c, p, pl.ds(0, 1), :], lambda p: ep[p, pl.ds(0, 1), :])

    pl.semaphore_wait(barrier, 18)

    def halo(core_at):
        rows = pl.ds(16 * core_at, 16)
        return [
            remote(cons.at[:, core, rows], qg.at[other], halo_send.at[core_at, 0],
                   halo_recv.at[other, 0], dev(chip + 2 * core - 1, core_at)),
            remote(phase.at[core, rows], pg.at[other], halo_send.at[core_at, 1],
                   halo_recv.at[other, 1], dev(chip + 2 * core - 1, core_at)),
        ]

    sends_halo = jnp.where(core == 0, chip > 0, chip < CHIPS - 1)

    @pl.when(sends_halo)
    def _():
        for core_at in range(2):
            for copy in halo(core_at):
                copy.start()

    peer = dev(chip, other)
    peer_rows = pl.ds(pl.multiple_of(8 * other, 8), 24)
    peer_dst = pl.ds(pl.multiple_of(8 * core, 8), 24)
    theirs = pl.ds(2 * other, 2)
    swaps = [
        remote(cons.at[:, :, peer_rows], qp.at[:, mine, peer_dst], chip_send.at[0], chip_recv.at[0], peer),
        remote(phase.at[:, peer_rows], pp.at[mine, peer_dst], chip_send.at[1], chip_recv.at[1], peer),
        remote(diag.at[:, :, :, other_half], dv.at[:, :, mine], chip_send.at[2], chip_recv.at[2], peer),
    ]
    swaps[0].start()
    swaps[1].start()
    row_copies = [
        remote(row_out.at[0], row_in.at[core], row_send.at[0], row_recv.at[core], dev(chip, 0, span_up)),
        remote(row_out.at[1], row_in.at[core], row_send.at[1], row_recv.at[core], dev(chip, 1, span_down)),
    ]
    for copy in row_copies:
        copy.start()
    swaps[2].start()

    swaps[0].wait_recv()
    swaps[1].wait_recv()
    for core_at in range(2):
        remote(row_out.at[0], row_in.at[core_at], row_send.at[0], row_recv.at[core_at], peer).wait_recv()
    ghost_row = 7 + 17 * core
    for core_at in range(2):
        for plane in range(2):
            for ch in range(5):
                qp[ch, 2 * core_at + plane, pl.ds(ghost_row, 1), :] = row_in[
                    core_at, pl.ds(ch * 2 + plane, 1), :
                ]
            pp[2 * core_at + plane, pl.ds(ghost_row, 1), :] = row_in[
                core_at, pl.ds(10 + plane, 1), :
            ].astype(jnp.int32)

    @pl.loop(0, 16)
    def _(step):
        plane = step // 4
        rows = pl.ds(pl.multiple_of((step % 4) * 8, 8), 8)
        fields = primitives([qp[ch, plane, rows, :] for ch in range(5)], pp[plane, rows, :])
        for ch in range(7):
            prim[ch, plane + 1, rows, :] = fields[ch]
        prim[7, plane + 1, rows, :] = 0.5 * (jnp.abs(fields[1]) + fields[6])

    def tile(q):
        return (
            pl.ds(pl.multiple_of((q // 4) * 8, 8), 8),
            pl.ds(pl.multiple_of((q % 4) * 128, 128), 128),
        )

    def weight(plane, q):
        return prim[
            7, plane + 1,
            pl.ds(pl.multiple_of((q // 4) * 8 + 8, 8), 8),
            pl.ds(pl.multiple_of((q % 4) * 128, 128), 128),
        ]

    def block(plane, q):
        rows, lanes = tile(q)
        return lambda i, j: dv[i, j, plane, rows, lanes]

    is_solver = core == SOLVER

    loads[4].wait()
    swaps[2].wait_recv()

    def chip_product(q, order):
        prod = None
        for plane in order:
            mat = block(plane, q)
            w = weight(plane, q)
            if prod is None:
                prod = [[mat(i, j) * w for j in range(5)] for i in range(5)]
            else:
                cols = [
                    matvec(mat, [prod[i][j] for i in range(5)]) for j in range(5)
                ]
                prod = [[cols[j][i] * w for j in range(5)] for i in range(5)]
        return prod

    inner = jnp.logical_and(chip > 0, chip < CHIPS - 1)

    def send_products(out, gathered, send, recv, order):
        @pl.loop(0, CHIPS)
        def _(step):
            q = xor_chip(chip, CHIPS - 1 - step)
            prod = chip_product(q, order)
            for i in range(5):
                for j in range(5):
                    out[q, i, j] = prod[i][j]
            to_self = jnp.logical_and(is_solver, q == chip)

            @pl.when(jnp.logical_not(to_self))
            def _():
                remote(out.at[q], gathered.at[core, chip], send.at[q], recv.at[core, chip],
                       dev(q, SOLVER)).start()

            @pl.when(to_self)
            def _():
                gathered[core, chip] = out[q]

    @pl.when(inner)
    def _():
        send_products(m_out, m_all, m_send, m_recv, (0, 1, 2, 3))

    lane = lax.broadcasted_iota(jnp.int32, (8, 512), 1)

    @pl.loop(0, 8)
    def _(step):
        plane = step // 2
        rows = pl.ds(pl.multiple_of((step % 2) * 8 + 8, 8), 8)
        out_rows = pl.ds(pl.multiple_of((step % 2) * 8, 8), 8)
        cell = [prim[ch, plane + 1, rows, :] for ch in range(7)]
        below = []
        for ch in range(7):
            first = -cell[ch] if ch == 3 else cell[ch]
            below.append(jnp.where(lane == 0, first, pltpu.roll(cell[ch], 1, axis=1)))
        low = hllc(below, cell, 3)
        mass = cell[0] * cell[3]
        top = [
            mass, cell[1] * mass, cell[2] * mass, cell[3] * mass + cell[5],
            cell[4] * mass + cell[5] * cell[3],
        ]
        for ch in range(5):
            high = jnp.where(lane == 511, top[ch], pltpu.roll(low[ch], 511, axis=1))
            acc[ch, plane, out_rows, :] = high - low[ch]

    @pl.loop(0, 16)
    def _(step):
        plane = step // 4
        lanes = pl.ds(pl.multiple_of((step % 4) * 128, 128), 128)
        down = [prim[ch, plane + 1, pl.ds(7, 24), lanes] for ch in range(7)]
        cell = [prim[ch, plane + 1, pl.ds(8, 24), lanes] for ch in range(7)]
        low = hllc(down, cell, 2)
        for ch in range(5):
            high = pltpu.roll(low[ch], 23, axis=0)
            acc[ch, plane, :, lanes] = acc[ch, plane, :, lanes] + (high - low[ch])[:16]

    @pl.when(chip == 0)
    def _():
        for ch in range(7):
            prim[ch, 0, pl.ds(8, 16), :] = prim[ch, 1, pl.ds(8, 16), :]

    @pl.when(chip == CHIPS - 1)
    def _():
        for ch in range(7):
            prim[ch, 5, pl.ds(8, 16), :] = prim[ch, 4, pl.ds(8, 16), :]

    def take_halo(side):
        remote(cons.at[:, 0, pl.ds(0, 16)], qg.at[side], halo_send.at[0, 0], halo_recv.at[side, 0], peer).wait_recv()
        remote(phase.at[0, pl.ds(0, 16)], pg.at[side], halo_send.at[0, 1], halo_recv.at[side, 1], peer).wait_recv()

        @pl.loop(0, 2)
        def _(part):
            rows = pl.ds(pl.multiple_of(part * 8, 8), 8)
            fields = primitives([qg[side, ch, rows, :] for ch in range(5)], pg[side, rows, :])
            for ch in range(7):
                prim[ch, 5 * side, pl.ds(pl.multiple_of(part * 8 + 8, 8), 8), :] = fields[ch]

    @pl.when(chip > 0)
    def _():
        take_halo(0)

    @pl.when(chip < CHIPS - 1)
    def _():
        take_halo(1)

    @pl.loop(0, CHIPS)
    def _(step):
        q = xor_chip(chip, CHIPS - 1 - step)
        rows, lanes = tile(q)
        prim_rows = pl.ds(pl.multiple_of((q // 4) * 8 + 8, 8), 8)
        states = lambda plane: [prim[ch, plane, prim_rows, lanes] for ch in range(7)]
        low = hllc(states(0), states(1), 1)
        flow = None
        for plane in range(4):
            high = hllc(states(plane + 1), states(plane + 2), 1)
            entry = []
            for ch in range(5):
                value = face_area * (acc[ch, plane, rows, lanes] + (high[ch] - low[ch]))
                res[ch, plane, rows, lanes] = value
                entry.append(-value if flow is None else flow[ch] - value)
            low = high
            w = weight(plane, q)
            flow = [w * value for value in matvec(block(plane, q), entry)]

        for ch in range(5):
            g_out[q, ch] = flow[ch]
        to_self = jnp.logical_and(is_solver, q == chip)

        @pl.when(jnp.logical_and(jnp.logical_not(to_self), chip < CHIPS - 1))
        def _():
            remote(g_out.at[q], g_all.at[core, chip], g_send.at[q], g_recv.at[core, chip],
                   dev(q, SOLVER)).start()

        @pl.when(to_self)
        def _():
            g_all[core, chip] = g_out[q]

    out_copies = [
        pltpu.make_async_copy(res.at[:, mine], resid.at[:, :, half], out_sem.at[0]),
        remote(res.at[:, theirs], resid.at[:, :, half], out_send.at[0], out_recv.at[0], peer),
    ]
    for copy in out_copies:
        copy.start()

    @pl.when(inner)
    def _():
        send_products(n_out, n_all, n_send, n_recv, (3, 2, 1, 0))

    def gather_wait(gathered, recv, src_chip):
        for src_core in range(2):
            def wait():
                remote(gathered.at[src_core, src_chip], gathered.at[src_core, src_chip],
                       recv.at[src_core, src_chip], recv.at[src_core, src_chip], peer).wait_recv()

            if src_core == SOLVER:
                pl.when(chip != src_chip)(wait)
            else:
                wait()

    def scatter(values, out, landed, send, recv, to_chip):
        for to_core in range(2):
            for ch in range(5):
                out[to_core, to_chip, ch] = values[to_core][ch]

            def start():
                remote(out.at[to_core, to_chip], landed.at[chip], send.at[to_core, to_chip],
                       recv.at[chip], dev(to_chip, to_core)).start()

            if to_core == SOLVER:
                pl.when(chip != to_chip)(start)

                @pl.when(chip == to_chip)
                def _():
                    for ch in range(5):
                        landed[chip, ch] = values[to_core][ch]
            else:
                start()

    def recurrence(mats, mats_recv, vecs, vecs_recv, out, landed, send, recv, order):
        flow = None
        for at, src in enumerate(order[:-1]):
            gather_wait(vecs, vecs_recv, src)
            new = []
            if at > 0:
                gather_wait(mats, mats_recv, src)
            for a in range(2):
                value = [vecs[a, src, ch] for ch in range(5)]
                if at > 0:
                    moved = matvec(lambda i, j: mats[a, src, i, j], flow[a])
                    value = [x + y for x, y in zip(value, moved)]
                new.append(value)
            flow = new
            scatter(flow, out, landed, send, recv, order[at + 1])

    @pl.when(is_solver)
    def _():
        recurrence(m_all, m_recv, g_all, g_recv, f_out, f_all, f_send, f_recv, tuple(range(CHIPS)))

    def landed_wait(landed, recv, q):
        @pl.when(jnp.logical_not(jnp.logical_and(is_solver, q == chip)))
        def _():
            remote(landed.at[q], landed.at[q], recv.at[q], recv.at[q], peer).wait_recv()

    @pl.when(chip == 0)
    def _():
        f_all[...] = jnp.zeros_like(f_all)

    @pl.loop(0, CHIPS)
    def _(step):
        q = xor_chip(chip, step)
        rows, lanes = tile(q)

        @pl.when(chip > 0)
        def _():
            landed_wait(f_all, f_recv, q)

        flow = [f_all[q, ch] for ch in range(5)]
        sweep = []
        for plane in range(4):
            entry = [flow[ch] - res[ch, plane, rows, lanes] for ch in range(5)]
            value = matvec(block(plane, q), entry)
            sweep.append(value)
            for ch in range(5):
                swp[ch, plane, rows, lanes] = value[ch]
            w = weight(plane, q)
            flow = [w * x for x in value]
        for plane in (2, 1, 0):
            moved = matvec(block(plane, q), flow)
            w = weight(plane, q)
            flow = [w * (x + y) for x, y in zip(sweep[plane], moved)]
        for ch in range(5):
            h_out[q, ch] = flow[ch]
        to_self = jnp.logical_and(is_solver, q == chip)

        @pl.when(jnp.logical_and(jnp.logical_not(to_self), chip > 0))
        def _():
            remote(h_out.at[q], h_all.at[core, chip], h_send.at[q], h_recv.at[core, chip],
                   dev(q, SOLVER)).start()

        @pl.when(to_self)
        def _():
            h_all[core, chip] = h_out[q]

    @pl.when(is_solver)
    def _():
        recurrence(n_all, n_recv, h_all, h_recv, w_out, w_all, w_send, w_recv,
                   tuple(range(CHIPS - 1, -1, -1)))

    @pl.when(chip == CHIPS - 1)
    def _():
        w_all[...] = jnp.zeros_like(w_all)

    @pl.loop(0, CHIPS)
    def _(step):
        q = xor_chip(chip, step)
        rows, lanes = tile(q)

        @pl.when(chip < CHIPS - 1)
        def _():
            landed_wait(w_all, w_recv, q)

        flow = [w_all[q, ch] for ch in range(5)]
        for plane in (3, 2, 1, 0):
            moved = matvec(block(plane, q), flow)
            value = [swp[ch, plane, rows, lanes] + moved[ch] for ch in range(5)]
            for ch in range(5):
                upv[ch, plane, rows, lanes] = value[ch]
            w = weight(plane, q)
            flow = [w * x for x in value]

    final = [
        pltpu.make_async_copy(upv.at[:, mine], upd.at[:, :, half], out_sem.at[1]),
        remote(upv.at[:, theirs], upd.at[:, :, half], out_send.at[1], out_recv.at[1], peer),
    ]
    for copy in final:
        copy.start()

    for copy in swaps:
        copy.wait_send()
    for copy in row_copies:
        copy.wait_send()

    @pl.when(sends_halo)
    def _():
        for core_at in range(2):
            for copy in halo(core_at):
                copy.wait_send()

    @pl.loop(0, CHIPS)
    def _(q):
        not_self = jnp.logical_not(jnp.logical_and(is_solver, q == chip))

        def drain(out, gathered, send, recv, when):
            @pl.when(jnp.logical_and(not_self, when))
            def _():
                remote(out.at[q], gathered.at[core, chip], send.at[q], recv.at[core, chip], peer).wait_send()

        drain(m_out, m_all, m_send, m_recv, inner)
        drain(n_out, n_all, n_send, n_recv, inner)
        drain(g_out, g_all, g_send, g_recv, chip < CHIPS - 1)
        drain(h_out, h_all, h_send, h_recv, chip > 0)

    @pl.when(is_solver)
    def _():
        def drain(out, landed, send, recv, to_chip):
            for to_core in range(2):
                def wait():
                    remote(out.at[to_core, to_chip], landed.at[chip], send.at[to_core, to_chip],
                           recv.at[chip], peer).wait_send()

                if to_core == SOLVER:
                    pl.when(chip != to_chip)(wait)
                else:
                    wait()

        for to_chip in range(1, CHIPS):
            drain(f_out, f_all, f_send, f_recv, to_chip)
        for to_chip in range(CHIPS - 1):
            drain(w_out, w_all, w_send, w_recv, to_chip)

    out_copies[0].wait()
    out_copies[1].wait()
    final[0].wait()
    final[1].wait()


def body(cons, phase, diag):
    dma = pltpu.SemaphoreType.DMA
    vm = lambda *shape: pltpu.VMEM(shape, f32)
    vi = lambda *shape: pltpu.VMEM(shape, jnp.int32)
    per_chip = lambda *shape: vm(CHIPS, *shape, 8, 128)
    scratch = [
        vm(5, 4, 32, 512), vi(4, 32, 512), vm(2, 5, 16, 512), vi(2, 16, 512),
        vm(5, 2, 8, 512), vi(2, 8, 512), vm(2, 16, 512), vm(2, 16, 512),
        vm(5, 5, 4, 16, 512), vm(8, 6, 32, 512),
        vm(5, 4, 16, 512), vm(5, 4, 16, 512), vm(5, 4, 16, 512), vm(5, 4, 16, 512),
        per_chip(5, 5), per_chip(5, 5), vm(2, CHIPS, 5, 5, 8, 128), vm(2, CHIPS, 5, 5, 8, 128),
        per_chip(5), vm(2, CHIPS, 5, 8, 128), vm(2, CHIPS, 5, 8, 128), per_chip(5),
        per_chip(5), vm(2, CHIPS, 5, 8, 128), vm(2, CHIPS, 5, 8, 128), per_chip(5),
        dma((5,)), dma((3,)), dma((3,)), dma((2, 2)), dma((2, 2)), dma((2,)), dma((2,)),
        dma((CHIPS,)), dma((2, CHIPS)), dma((CHIPS,)), dma((2, CHIPS)),
        dma((CHIPS,)), dma((2, CHIPS)), dma((2, CHIPS)), dma((CHIPS,)),
        dma((CHIPS,)), dma((2, CHIPS)), dma((2, CHIPS)), dma((CHIPS,)),
        dma((2,)), dma((2,)), dma((2,)),
    ]
    out = jax.ShapeDtypeStruct(cons.shape, f32)
    anywhere = pl.BlockSpec(memory_space=pl.ANY)
    return pl.pallas_call(
        kernel,
        out_shape=(out, out),
        in_specs=[anywhere] * 3,
        out_specs=(anywhere, anywhere),
        scratch_shapes=scratch,
        compiler_params=pltpu.CompilerParams(
            collective_id=0, has_side_effects=True, vmem_limit_bytes=40 * 2**20
        ),
        name="flow_sweep",
    )(cons, phase, diag)


def solution(mesh):
    in_specs = (
        P(None, "stream", "span", None),
        P("stream", "span", None),
        P(None, None, "stream", "span", None),
    )
    out_specs = (P(None, "stream", "span", None), P(None, "stream", "span", None))
    return jax.shard_map(body, mesh=mesh, in_specs=in_specs, out_specs=out_specs, check_vma=False)
```

```python
import jax
import jax.numpy as jnp
from jax import lax
from jax.experimental import pallas as pl
from jax.experimental.pallas import tpu as pltpu
from jax.sharding import PartitionSpec as P

face_area = 0.0625
MESH = pl.DeviceIdType.MESH
CHIPS = 8
SOLVER = 1
f32 = jnp.float32


def eos(phase):
    ratio = jnp.where(phase == 0, 4.4, jnp.where(phase == 1, 1.4, 2.0)).astype(f32)
    stiff = jnp.where(phase == 0, 1.0, jnp.where(phase == 1, 0.0, 0.5)).astype(f32)
    return ratio, stiff


def primitives(cons, phase):
    ratio, stiff = eos(phase)
    density = cons[0]
    inverse = 1.0 / density
    u1, u2, u3 = cons[1] * inverse, cons[2] * inverse, cons[3] * inverse
    kinetic = 0.5 * density * (u1 * u1 + u2 * u2 + u3 * u3)
    pressure = (ratio - 1.0) * (cons[4] - kinetic) - ratio * stiff
    sound = jnp.sqrt(ratio * (pressure + stiff) * inverse)
    return [density, u1, u2, u3, cons[4] * inverse, pressure, sound]


def hllc(left, right, normal):
    ql, qr = left[normal], right[normal]
    cl, cr = left[6], right[6]
    sl = jnp.minimum(ql - cl, qr - cr)
    sr = jnp.maximum(ql + cl, qr + cr)
    ml = left[0] * (sl - ql)
    mr = right[0] * (sr - qr)
    contact = (right[5] - left[5] + ml * ql - mr * qr) / (ml - mr)
    supersonic = sl >= 0.0
    ahead = contact >= 0.0
    use_left = jnp.logical_or(supersonic, ahead)
    starred = jnp.logical_and(
        jnp.logical_not(supersonic), jnp.logical_or(ahead, sr >= 0.0)
    )
    pick = lambda a, b: jnp.where(use_left, a, b)
    s, m, q = pick(sl, sr), pick(ml, mr), pick(ql, qr)
    p, e = pick(left[5], right[5]), pick(left[4], right[4])
    ss = jnp.where(starred, contact, q)
    inv = 1.0 / (s - ss)
    mass = m * inv * ss
    out = [mass]
    for d in (1, 2, 3):
        if d == normal:
            out.append(s * mass - q * m + p)
        else:
            out.append(pick(left[d], right[d]) * mass)
    out.append(p * q + e * mass + s * (ss - q) * (mass + p * inv))
    return out


def matvec(mat, vec):
    return [
        mat(i, 0) * vec[0]
        + mat(i, 1) * vec[1]
        + mat(i, 2) * vec[2]
        + mat(i, 3) * vec[3]
        + mat(i, 4) * vec[4]
        for i in range(5)
    ]


def kernel(
    cons, phase, diag, upd, resid,
    qo, po, qp, pp, qg, pg, row_out, row_in, wo, do, dv, prim, acc, swp, res, upv, hloc,
    mx, nx, pm, pn, km, m_out, n_out, m_all, n_all,
    g_out, g_all, f_out, f_all, h_out, h_all, w_out, w_all,
    loc_sem, chip_send, chip_recv, mx_recv, halo_send, halo_recv, row_send, row_recv,
    sent, nx_recv, m_recv, n_recv, g_recv, h_recv, f_recv, w_recv, out_sem, out_send, out_recv,
):
    stream = lax.axis_index("stream")
    span = lax.axis_index("span")
    spans = lax.axis_size("span")
    core = stream % 2
    chip = stream // 2
    other = 1 - core
    bits = (chip // 4, (chip // 2) % 2, chip % 2)
    span_up = (span + 1) % spans
    span_down = (span + spans - 1) % spans
    is_solver = core == SOLVER
    mx_send, nx_send, m_send, n_send, g_send, h_send, f_send, w_send = [sent.at[k] for k in range(8)]
    inner = jnp.logical_and(chip > 0, chip < CHIPS - 1)

    def dev(chip_at, core_at, span_at=None):
        return {
            "stream": chip_at * 2 + core_at,
            "span": span if span_at is None else span_at,
        }

    def remote(src, dst, send, recv, device):
        return pltpu.make_async_remote_copy(
            src_ref=src, dst_ref=dst, send_sem=send, recv_sem=recv,
            device_id=device, device_id_type=MESH,
        )

    def flip(bit, by):
        return bit + by - 2 * bit * by

    def aligned(value, by):
        return pl.multiple_of(value, by)

    def each_chip(run, near_first=False, halves=(0, 1), quarters=(0, 1)):
        turn = (lambda i: i) if near_first else (lambda i: 1 - i)

        @pl.loop(halves[0], halves[-1] + 1)
        def _(a):
            rb = flip(bits[0], turn(a))

            @pl.loop(quarters[0], quarters[-1] + 1)
            def _(b):
                l2 = flip(bits[1], turn(b))

                @pl.loop(0, 2)
                def _(c):
                    lb = l2 * 2 + flip(bits[2], turn(c))
                    run(rb * 4 + lb, rb, lb)

    peer = dev(chip, other)

    mine = pl.ds(2 * core, 2)
    theirs = pl.ds(2 * other, 2)
    half = pl.ds(aligned(16 * core, 16), 16)
    other_half = pl.ds(aligned(16 * other, 16), 16)
    loads = [
        pltpu.make_async_copy(cons, qo, loc_sem.at[0]),
        pltpu.make_async_copy(phase, po, loc_sem.at[1]),
        pltpu.make_async_copy(diag.at[:, :, :, other_half], do, loc_sem.at[2]),
        pltpu.make_async_copy(diag.at[:, :, :, half], dv.at[:, :, mine], loc_sem.at[3]),
        pltpu.make_async_copy(
            cons.at[:, :, pl.ds(aligned(8 * core, 8), 24)],
            qp.at[:, mine, pl.ds(aligned(8 * other, 8), 24)], loc_sem.at[4]),
        pltpu.make_async_copy(
            phase.at[:, pl.ds(aligned(8 * core, 8), 24)],
            pp.at[mine, pl.ds(aligned(8 * other, 8), 24)], loc_sem.at[5]),
    ]
    for copy in loads:
        copy.start()

    barrier = pltpu.get_barrier_semaphore()

    def greet(device):
        pl.semaphore_signal(barrier, inc=1, device_id=device, device_id_type=MESH)

    span_near = core * span_up + other * span_down
    span_far = core * span_down + other * span_up
    greet(dev(chip, core, span_near))
    greet(dev(chip, other, span_near))
    greet(dev(chip, core, span_far))
    for k in range(7, -1, -1):
        at = [flip(bits[n], (k >> (2 - n)) & 1) for n in range(3)]
        to = at[0] * 4 + at[1] * 2 + at[2]
        greet(dev(to, other))
        if k:
            greet(dev(to, core))

    loads[0].wait()
    loads[1].wait()
    for side, at in ((0, 31), (1, 0)):
        for ch in range(5):
            for plane in range(2):
                row_out[side, pl.ds(ch * 2 + plane, 1), :] = qo[ch, plane, pl.ds(at, 1), :]
        for plane in range(2):
            row_out[side, pl.ds(10 + plane, 1), :] = po[plane, pl.ds(at, 1), :].astype(f32)
        row_out[side, pl.ds(12, 4), :] = jnp.zeros((4, 512), f32)

    @pl.loop(0, 2)
    def _(plane):
        @pl.loop(0, 4)
        def _(part):
            rows = pl.ds(aligned(part * 8, 8), 8)
            fields = primitives([qo[ch, plane, rows, :] for ch in range(5)], po[plane, rows, :])
            wo[plane, rows, :] = 0.5 * (jnp.abs(fields[1]) + fields[6])

    def weighted(mat, w):
        return [[mat(i, j) * w for j in range(5)] for i in range(5)]

    def product(mat, right, w=None):
        cols = [matvec(mat, [right[i][j] for i in range(5)]) for j in range(5)]
        return [[cols[j][i] if w is None else cols[j][i] * w for j in range(5)] for i in range(5)]

    def put(ref, at, prod):
        for i in range(5):
            for j in range(5):
                ref[(*at, i, j)] = prod[i][j]

    def own_products(half_at, mat_of, m_at, n_at):
        def run(q, rb, lb):
            rows = pl.ds(aligned(rb * 8, 8), 8)
            lanes = pl.ds(aligned(lb * 128, 128), 128)
            w_rows = pl.ds(aligned(half_at * 16 + rb * 8, 8), 8)
            w = [wo[plane, w_rows, lanes] for plane in range(2)]
            mats = [
                (lambda i, j, plane=plane: mat_of(i, j, plane, rows, lanes)) for plane in range(2)
            ]
            put(m_at[0], (*m_at[1], q), product(mats[1], weighted(mats[0], w[0]), w[1]))
            put(n_at[0], (*n_at[1], q), product(mats[0], weighted(mats[1], w[1]), w[0]))

        each_chip(run)

    loads[2].wait()
    own_products(other, lambda i, j, p, r, l: do[i, j, p, r, l], (mx, ()), (nx, ()))
    loads[3].wait()
    own_products(core, lambda i, j, p, r, l: dv[i, j, 2 * core + p, r, l], (pm, (core,)), (pn, (core,)))
    loads[4].wait()
    loads[5].wait()

    pl.semaphore_wait(barrier, 18)

    ahead = chip + 2 * core - 1

    def halo(core_at, part):
        rb = flip(bits[0], 1 - part)
        src = pl.ds(aligned(16 * core_at + 8 * rb, 8), 8)
        dst = pl.ds(aligned(8 * rb, 8), 8)
        return [
            remote(qo.at[:, core, src], qg.at[other, :, dst], halo_send.at[0],
                   halo_recv.at[other, rb, 0], dev(ahead, core_at)),
            remote(po.at[core, src], pg.at[other, dst], halo_send.at[1],
                   halo_recv.at[other, rb, 1], dev(ahead, core_at)),
        ]

    sends_halo = jnp.logical_or(
        jnp.logical_and(core == 0, chip > 0), jnp.logical_and(core == 1, chip < CHIPS - 1)
    )


    peer_rows = pl.ds(aligned(8 * other, 8), 24)
    peer_dst = pl.ds(aligned(8 * core, 8), 24)
    swaps = [
        remote(qo.at[:, :, peer_rows], qp.at[:, mine, peer_dst], chip_send.at[0], chip_recv.at[0], peer),
        remote(po.at[:, peer_rows], pp.at[mine, peer_dst], chip_send.at[1], chip_recv.at[1], peer),
        remote(do, dv.at[:, :, mine], chip_send.at[2], chip_recv.at[2], peer),
    ]
    row_copies = [
        remote(row_out.at[0], row_in.at[core], row_send.at[0], row_recv.at[core], dev(chip, 0, span_up)),
        remote(row_out.at[1], row_in.at[core], row_send.at[1], row_recv.at[core], dev(chip, 1, span_down)),
    ]

    def mx_copy(q):
        return remote(mx.at[q], pm.at[core, q], mx_send, mx_recv.at[q], peer)

    def nx_copy():
        return remote(nx, pn.at[core], nx_send, nx_recv.at[0], peer)

    for copy in row_copies:
        copy.start()

    @pl.when(sends_halo)
    def _():
        for part in range(2):
            for core_at in range(2):
                for copy in halo(core_at, part):
                    copy.start()

    @pl.when(inner)
    def _():
        each_chip(lambda q, rb, lb: mx_copy(q).start())

    swaps[0].start()
    swaps[1].start()

    def slot(core_at, chip_at):
        return core_at * CHIPS + chip_at

    def to_solver(q, out, gathered, send, recv, when=None):
        to_self = jnp.logical_and(is_solver, q == chip)
        goes = jnp.logical_not(to_self)

        @pl.when(goes if when is None else jnp.logical_and(goes, when))
        def _():
            remote(out.at[q], gathered.at[slot(core, chip)], send, recv.at[0], dev(q, SOLVER)).start()

        @pl.when(to_self)
        def _():
            gathered[slot(core, chip)] = out[q]

    def chip_product(parts, left, right, out, q):
        mat = lambda i, j: parts[left, q, i, j]
        right_mat = [[parts[right, q, i, j] for j in range(5)] for i in range(5)]
        put(out, (q,), product(mat, right_mat))

    @pl.when(inner)
    def _():
        def run(q, rb, lb):
            mx_copy(q).wait_recv()
            chip_product(pm, 1, 0, m_out, q)
            to_solver(q, m_out, m_all, m_send, m_recv)

        each_chip(run)
        nx_copy().start()

    swaps[2].start()

    def send_n(half_at, quarters=(0, 1)):
        def run(q, rb, lb):
            chip_product(pn, 0, 1, n_out, q)
            to_solver(q, n_out, n_all, n_send, n_recv)

        @pl.when(inner)
        def _():
            each_chip(run, halves=(half_at,), quarters=quarters)

    def set_primitives(plane, first):
        rows = pl.ds(aligned(first, 8), 8)
        fields = primitives([qp[ch, plane, rows, :] for ch in range(5)], pp[plane, rows, :])
        for ch in range(7):
            prim[ch, plane + 1, rows, :] = fields[ch]
        prim[7, plane + 1, rows, :] = 0.5 * (jnp.abs(fields[1]) + fields[6])

    swaps[0].wait_recv()
    swaps[1].wait_recv()

    @pl.loop(0, 4)
    def _(plane):
        @pl.loop(0, 3)
        def _(part):
            set_primitives(plane, 8 * (other + part))

    lane = lax.broadcasted_iota(jnp.int32, (8, 512), 1)

    @pl.loop(0, 4)
    def _(plane):
        @pl.loop(0, 2)
        def _(part):
            rows = pl.ds(aligned(part * 8 + 8, 8), 8)
            out_rows = pl.ds(aligned(part * 8, 8), 8)
            cell = [prim[ch, plane + 1, rows, :] for ch in range(7)]
            below = []
            for ch in range(7):
                first = -cell[ch] if ch == 3 else cell[ch]
                below.append(jnp.where(lane == 0, first, pltpu.roll(cell[ch], 1, axis=1)))
            low = hllc(below, cell, 3)
            mass = cell[0] * cell[3]
            top = [
                mass, cell[1] * mass, cell[2] * mass, cell[3] * mass + cell[5],
                cell[4] * mass + cell[5] * cell[3],
            ]
            for ch in range(5):
                high = jnp.where(lane == 511, top[ch], pltpu.roll(low[ch], 511, axis=1))
                acc[ch, plane, out_rows, :] = high - low[ch]

    @pl.loop(0, 2)
    def _(part):
        rows = pl.ds(aligned(part * 8 + 8, 8), 8)
        out_rows = pl.ds(aligned(part * 8, 8), 8)

        @pl.loop(0, 3)
        def _(plane):
            states = lambda p: [prim[ch, p, rows, :] for ch in range(7)]
            face = hllc(states(plane + 1), states(plane + 2), 1)
            for ch in range(5):
                acc[ch, plane, out_rows, :] = acc[ch, plane, out_rows, :] + face[ch]
                acc[ch, plane + 1, out_rows, :] = acc[ch, plane + 1, out_rows, :] - face[ch]

    for core_at in range(2):
        remote(row_out.at[0], row_in.at[core_at], row_send.at[0], row_recv.at[core_at], peer).wait_recv()
    ghost_row = 7 + 17 * core
    for core_at in range(2):
        for plane in range(2):
            for ch in range(5):
                qp[ch, 2 * core_at + plane, pl.ds(ghost_row, 1), :] = row_in[
                    core_at, pl.ds(ch * 2 + plane, 1), :
                ]
            pp[2 * core_at + plane, pl.ds(ghost_row, 1), :] = row_in[
                core_at, pl.ds(10 + plane, 1), :
            ].astype(jnp.int32)

    @pl.loop(0, 4)
    def _(plane):
        set_primitives(plane, 24 * core)

    @pl.loop(0, 4)
    def _(plane):
        @pl.loop(0, 4)
        def _(part):
            lanes = pl.ds(aligned(part * 128, 128), 128)
            down = [prim[ch, plane + 1, pl.ds(7, 24), lanes] for ch in range(7)]
            cell = [prim[ch, plane + 1, pl.ds(8, 24), lanes] for ch in range(7)]
            low = hllc(down, cell, 2)
            for ch in range(5):
                high = pltpu.roll(low[ch], 23, axis=0)
                acc[ch, plane, :, lanes] = acc[ch, plane, :, lanes] + (high - low[ch])[:16]

    def block(plane, rb, lb):
        rows = pl.ds(aligned(rb * 8, 8), 8)
        lanes = pl.ds(aligned(lb * 128, 128), 128)
        return lambda i, j: dv[i, j, plane, rows, lanes]

    def weight(plane, rb, lb):
        return prim[7, plane + 1, pl.ds(aligned(rb * 8 + 8, 8), 8), pl.ds(aligned(lb * 128, 128), 128)]

    def cells(ref, plane, rb, lb):
        rows = pl.ds(aligned(rb * 8, 8), 8)
        lanes = pl.ds(aligned(lb * 128, 128), 128)
        return [ref[ch, plane, rows, lanes] for ch in range(5)]

    def set_cells(ref, plane, rb, lb, values):
        rows = pl.ds(aligned(rb * 8, 8), 8)
        lanes = pl.ds(aligned(lb * 128, 128), 128)
        for ch in range(5):
            ref[ch, plane, rows, lanes] = values[ch]

    def edge_face(side, rb):
        rows = pl.ds(aligned(rb * 8 + 8, 8), 8)
        out_rows = pl.ds(aligned(rb * 8, 8), 8)
        inside = [prim[ch, 1 + 3 * side, rows, :] for ch in range(7)]

        def add(outside):
            face = hllc(outside, inside, 1) if side == 0 else hllc(inside, outside, 1)
            for ch in range(5):
                value = acc[ch, 3 * side, out_rows, :]
                acc[ch, 3 * side, out_rows, :] = value - face[ch] if side == 0 else value + face[ch]

        at_end = chip == (CHIPS - 1) * side

        @pl.when(at_end)
        def _():
            add(inside)

        @pl.when(jnp.logical_not(at_end))
        def _():
            dst = pl.ds(aligned(rb * 8, 8), 8)
            remote(qg.at[side, :, dst], qg.at[side, :, dst], halo_send.at[0],
                   halo_recv.at[side, rb, 0], peer).wait_recv()
            remote(pg.at[side, dst], pg.at[side, dst], halo_send.at[1],
                   halo_recv.at[side, rb, 1], peer).wait_recv()
            add(primitives([qg[side, ch, dst, :] for ch in range(5)], pg[side, dst, :]))

    swaps[2].wait_recv()

    for group in range(2):
        rb_at = flip(bits[0], 1 - group)
        for side in range(2):
            edge_face(side, rb_at)

        def local_forward(q, rb, lb):
            flow = None
            for plane in range(4):
                value = [face_area * x for x in cells(acc, plane, rb, lb)]
                set_cells(res, plane, rb, lb, value)
                entry = [-x for x in value] if flow is None else [y - x for x, y in zip(value, flow)]
                value = matvec(block(plane, rb, lb), entry)
                set_cells(swp, plane, rb, lb, value)
                w = weight(plane, rb, lb)
                flow = [w * x for x in value]
            for ch in range(5):
                g_out[q, ch] = flow[ch]
            to_solver(q, g_out, g_all, g_send, g_recv, chip < CHIPS - 1)

        each_chip(local_forward, halves=(group,))

    @pl.when(inner)
    def _():
        nx_copy().wait_recv()

    send_n(0, (0,))

    def response(q, rb, lb):
        blocks = [block(plane, rb, lb) for plane in range(4)]
        ws = [weight(plane, rb, lb) for plane in range(4)]

        def back(sweep):
            flow = [ws[3] * x for x in sweep[3]]
            for plane in (2, 1, 0):
                moved = matvec(blocks[plane], flow)
                flow = [ws[plane] * (x + y) for x, y in zip(sweep[plane], moved)]
            return flow

        local = back([cells(swp, plane, rb, lb) for plane in range(4)])
        for ch in range(5):
            hloc[q, ch] = local[ch]
        for j in range(5):
            sweep = [[blocks[0](i, j) for i in range(5)]]
            for plane in range(1, 4):
                sweep.append(matvec(blocks[plane], [ws[plane - 1] * x for x in sweep[-1]]))
            column = back(sweep)
            for i in range(5):
                km[q, i, j] = column[i]

    each_chip(response)

    def gather_wait(gathered, recv, total, fewer):
        @pl.when(fewer)
        def _():
            part = gathered.at[pl.ds(0, total - 1)]
            remote(part, part, sent.at[8], recv.at[0], peer).wait_recv()

        @pl.when(jnp.logical_not(fewer))
        def _():
            part = gathered.at[pl.ds(0, total)]
            remote(part, part, sent.at[8], recv.at[0], peer).wait_recv()

    def scatter(values, out, landed, send, recv, to_chip):
        for to_core in range(2):
            at = slot(to_core, to_chip)
            for ch in range(5):
                out[at, ch] = values[to_core][ch]

            def start():
                remote(out.at[at], landed.at[chip], send, recv.at[bits[0]], dev(to_chip, to_core)).start()

            if to_core == SOLVER:
                pl.when(chip != to_chip)(start)

                @pl.when(chip == to_chip)
                def _():
                    for ch in range(5):
                        landed[chip, ch] = values[to_core][ch]
            else:
                start()

    def recurrence(mats, vecs, out, landed, send, recv, order):
        flow = None
        for at, src in enumerate(order[:-1]):
            new = []
            for a in range(2):
                value = [vecs[slot(a, src), ch] for ch in range(5)]
                if at > 0:
                    moved = matvec(lambda i, j: mats[slot(a, src), i, j], flow[a])
                    value = [x + y for x, y in zip(value, moved)]
                new.append(value)
            flow = new
            scatter(flow, out, landed, send, recv, order[at + 1])

    @pl.when(is_solver)
    def _():
        gather_wait(m_all, m_recv, 2 * (CHIPS - 2), inner)
        gather_wait(g_all, g_recv, 2 * (CHIPS - 1), chip < CHIPS - 1)
        recurrence(m_all, g_all, f_out, f_all, f_send, f_recv, tuple(range(CHIPS)))
        send_n(0, (1,))
        send_n(1, (0,))


    def landed_wait(landed, recv, rb):
        fewer = jnp.logical_and(is_solver, rb == bits[0])

        @pl.when(fewer)
        def _():
            part = landed.at[pl.ds(0, 3)]
            remote(part, part, sent.at[8], recv.at[rb], peer).wait_recv()

        @pl.when(jnp.logical_not(fewer))
        def _():
            part = landed.at[pl.ds(0, 4)]
            remote(part, part, sent.at[8], recv.at[rb], peer).wait_recv()

    @pl.when(chip == 0)
    def _():
        f_all[...] = jnp.zeros_like(f_all)

    def backward_start(q, rb, lb):
        moved = matvec(lambda i, j: km[q, i, j], [f_all[q, ch] for ch in range(5)])
        for ch in range(5):
            h_out[q, ch] = hloc[q, ch] + moved[ch]
        to_solver(q, h_out, h_all, h_send, h_recv, chip > 0)

    for group in range(2):
        @pl.when(chip > 0)
        def _():
            landed_wait(f_all, f_recv, flip(bits[0], group))

        each_chip(backward_start, near_first=True, halves=(group,))

    @pl.when(jnp.logical_not(is_solver))
    def _():
        send_n(0, (1,))
        send_n(1, (0,))

    send_n(1, (1,))

    out_copies = [
        pltpu.make_async_copy(res.at[:, mine], resid.at[:, :, half], out_sem.at[0]),
        remote(res.at[:, theirs], resid.at[:, :, half], out_send.at[0], out_recv.at[0], peer),
    ]
    for copy in out_copies:
        copy.start()

    def both_sweeps(q, rb, lb):
        flow = [f_all[q, ch] for ch in range(5)]
        sweep = []
        for plane in range(4):
            entry = [y - x for x, y in zip(cells(res, plane, rb, lb), flow)]
            sweep.append(matvec(block(plane, rb, lb), entry))
            w = weight(plane, rb, lb)
            flow = [w * x for x in sweep[-1]]
        value = sweep[3]
        set_cells(swp, 3, rb, lb, value)
        for plane in (2, 1, 0):
            w = weight(plane + 1, rb, lb)
            moved = matvec(block(plane, rb, lb), [w * x for x in value])
            value = [x + y for x, y in zip(sweep[plane], moved)]
            set_cells(swp, plane, rb, lb, value)

    each_chip(both_sweeps)

    @pl.when(is_solver)
    def _():
        gather_wait(n_all, n_recv, 2 * (CHIPS - 2), inner)
        gather_wait(h_all, h_recv, 2 * (CHIPS - 1), chip > 0)
        recurrence(n_all, h_all, w_out, w_all, w_send, w_recv, tuple(range(CHIPS - 1, -1, -1)))

    @pl.when(chip == CHIPS - 1)
    def _():
        w_all[...] = jnp.zeros_like(w_all)

    def finish(q, rb, lb):
        flow = [w_all[q, ch] for ch in range(5)]
        for plane in (3, 2, 1, 0):
            moved = matvec(block(plane, rb, lb), flow)
            set_cells(upv, plane, rb, lb, [x + y for x, y in zip(cells(swp, plane, rb, lb), moved)])
            w = weight(plane, rb, lb)
            flow = [w * x for x in moved]

    def final(group):
        rb = flip(bits[0], group)
        src = pl.ds(aligned(8 * rb, 8), 8)
        dst = pl.ds(aligned(16 * core + 8 * rb, 8), 8)
        return [
            remote(upv.at[:, theirs, src], upd.at[:, :, dst], out_send.at[1 + group],
                   out_recv.at[1 + group], peer),
            pltpu.make_async_copy(upv.at[:, mine, src], upd.at[:, :, dst], out_sem.at[1 + group]),
        ]

    for group in range(2):
        @pl.when(chip < CHIPS - 1)
        def _():
            landed_wait(w_all, w_recv, flip(bits[0], group))

        each_chip(finish, near_first=True, halves=(group,))
        for copy in final(group):
            copy.start()

    for copy in swaps:
        copy.wait_send()
    for copy in row_copies:
        copy.wait_send()

    def drain(part, send):
        remote(part, part, send, nx_recv.at[0], peer).wait_send()

    @pl.when(sends_halo)
    def _():
        drain(qo.at[:, 0], halo_send.at[0])
        drain(po.at[0], halo_send.at[1])

    def drain_either(out, send, total, fewer, when):
        for less in (False, True):
            case = fewer if less else jnp.logical_not(fewer)

            @pl.when(case if when is None else jnp.logical_and(case, when))
            def _():
                drain(out.at[pl.ds(0, total - less)], send)

    @pl.when(inner)
    def _():
        drain(mx, mx_send)
        drain(nx, nx_send)

    drain_either(m_out, m_send, CHIPS, is_solver, inner)
    drain_either(n_out, n_send, CHIPS, is_solver, inner)
    drain_either(g_out, g_send, CHIPS, is_solver, chip < CHIPS - 1)
    drain_either(h_out, h_send, CHIPS, is_solver, chip > 0)
    drain_either(f_out, f_send, 2 * (CHIPS - 1), chip > 0, is_solver)
    drain_either(w_out, w_send, 2 * (CHIPS - 1), chip < CHIPS - 1, is_solver)

    out_copies[0].wait()
    out_copies[1].wait()
    for group in range(2):
        for copy in final(group):
            copy.wait()


def body(cons, phase, diag):
    dma = pltpu.SemaphoreType.DMA
    vm = lambda *shape: pltpu.VMEM(shape, f32)
    vi = lambda *shape: pltpu.VMEM(shape, jnp.int32)
    vecs = lambda *lead: vm(*lead, CHIPS, 5, 8, 128)
    mats = lambda *lead: vm(*lead, CHIPS, 5, 5, 8, 128)
    vecs2, mats2 = vm(2 * CHIPS, 5, 8, 128), vm(2 * CHIPS, 5, 5, 8, 128)
    scratch = [
        vm(5, 2, 32, 512), vi(2, 32, 512), vm(5, 4, 32, 512), vi(4, 32, 512),
        vm(2, 5, 16, 512), vi(2, 16, 512), vm(2, 16, 512), vm(2, 16, 512), vm(2, 32, 512),
        vm(5, 5, 2, 16, 512), vm(5, 5, 4, 16, 512), vm(8, 5, 32, 512),
        vm(5, 4, 16, 512), vm(5, 4, 16, 512), vm(5, 4, 16, 512), vm(5, 4, 16, 512), vecs(),
        mats(), mats(), mats(2), mats(2), mats(), mats(), mats(), mats2, mats2,
        vecs(), vecs2, vecs2, vecs(), vecs(), vecs2, vecs2, vecs(),
        dma((6,)), dma((3,)), dma((3,)), dma((CHIPS,)), dma((2,)), dma((2, 2, 2)), dma((2,)), dma((2,)),
        dma((9,)), dma((1,)), dma((1,)), dma((1,)), dma((1,)), dma((1,)), dma((2,)), dma((2,)),
        dma((3,)), dma((3,)), dma((3,)),
    ]
    out = jax.ShapeDtypeStruct(cons.shape, f32)
    anywhere = pl.BlockSpec(memory_space=pl.ANY)
    hbm = pl.BlockSpec(memory_space=pltpu.HBM)
    return pl.pallas_call(
        kernel,
        out_shape=(out, out),
        in_specs=[hbm] * 3,
        out_specs=(anywhere, anywhere),
        scratch_shapes=scratch,
        compiler_params=pltpu.CompilerParams(
            collective_id=0, has_side_effects=True, vmem_limit_bytes=60 * 2**20
        ),
        name="flow_sweep",
    )(cons, phase, diag)

def solution(mesh):
    in_specs = (
        P(None, "stream", "span", None),
        P("stream", "span", None),
        P(None, None, "stream", "span", None),
    )
    out_specs = (P(None, "stream", "span", None), P(None, "stream", "span", None))
    return jax.shard_map(body, mesh=mesh, in_specs=in_specs, out_specs=out_specs, check_vma=False)
```

```python
import jax
import jax.numpy as jnp
from jax import lax
from jax.experimental import pallas as pl
from jax.experimental.pallas import tpu as pltpu
from jax.sharding import PartitionSpec as P

face_area = 0.0625
MESH = pl.DeviceIdType.MESH
CHIPS = 8
SOLVER = 1
f32 = jnp.float32


def eos(phase):
    ratio = jnp.where(phase == 0, 4.4, jnp.where(phase == 1, 1.4, 2.0)).astype(f32)
    stiff = jnp.where(phase == 0, 1.0, jnp.where(phase == 1, 0.0, 0.5)).astype(f32)
    return ratio, stiff


def primitives(cons, phase):
    ratio, stiff = eos(phase)
    density = cons[0]
    inverse = 1.0 / density
    u1, u2, u3 = cons[1] * inverse, cons[2] * inverse, cons[3] * inverse
    kinetic = 0.5 * density * (u1 * u1 + u2 * u2 + u3 * u3)
    pressure = (ratio - 1.0) * (cons[4] - kinetic) - ratio * stiff
    sound = jnp.sqrt(ratio * (pressure + stiff) * inverse)
    return [density, u1, u2, u3, cons[4] * inverse, pressure, sound]


def hllc(left, right, normal):
    ql, qr = left[normal], right[normal]
    cl, cr = left[6], right[6]
    sl = jnp.minimum(ql - cl, qr - cr)
    sr = jnp.maximum(ql + cl, qr + cr)
    ml = left[0] * (sl - ql)
    mr = right[0] * (sr - qr)
    contact = (right[5] - left[5] + ml * ql - mr * qr) / (ml - mr)
    supersonic = sl >= 0.0
    ahead = contact >= 0.0
    use_left = jnp.logical_or(supersonic, ahead)
    starred = jnp.logical_and(
        jnp.logical_not(supersonic), jnp.logical_or(ahead, sr >= 0.0)
    )
    pick = lambda a, b: jnp.where(use_left, a, b)
    s, m, q = pick(sl, sr), pick(ml, mr), pick(ql, qr)
    p, e = pick(left[5], right[5]), pick(left[4], right[4])
    ss = jnp.where(starred, contact, q)
    inv = 1.0 / (s - ss)
    mass = m * inv * ss
    out = [mass]
    for d in (1, 2, 3):
        if d == normal:
            out.append(s * mass - q * m + p)
        else:
            out.append(pick(left[d], right[d]) * mass)
    out.append(p * q + e * mass + s * (ss - q) * (mass + p * inv))
    return out


def matvec(mat, vec):
    return [
        mat(i, 0) * vec[0]
        + mat(i, 1) * vec[1]
        + mat(i, 2) * vec[2]
        + mat(i, 3) * vec[3]
        + mat(i, 4) * vec[4]
        for i in range(5)
    ]


def kernel(
    cons, phase, diag, upd, resid,
    qo, po, qp, pp, qg, pg, row_out, row_in, wo, do, dv, prim, acc, swp, res, upv, hloc,
    mx, nx, pm, pn, km, m_out, n_out, m_all, n_all,
    g_out, g_all, f_out, f_all, h_out, h_all, w_out, w_all,
    loc_sem, chip_send, chip_recv, mx_recv, halo_send, halo_recv, row_send, row_recv,
    sent, nx_recv, m_recv, n_recv, g_recv, h_recv, f_recv, w_recv, out_sem, out_send, out_recv,
):
    stream = lax.axis_index("stream")
    span = lax.axis_index("span")
    spans = lax.axis_size("span")
    core = stream % 2
    chip = stream // 2
    other = 1 - core
    bits = (chip // 4, (chip // 2) % 2, chip % 2)
    span_up = (span + 1) % spans
    span_down = (span + spans - 1) % spans
    is_solver = core == SOLVER
    mx_send, nx_send, m_send, n_send, g_send, h_send, f_send, w_send = [sent.at[k] for k in range(8)]
    inner = jnp.logical_and(chip > 0, chip < CHIPS - 1)

    def dev(chip_at, core_at, span_at=None):
        return {
            "stream": chip_at * 2 + core_at,
            "span": span if span_at is None else span_at,
        }

    def remote(src, dst, send, recv, device):
        return pltpu.make_async_remote_copy(
            src_ref=src, dst_ref=dst, send_sem=send, recv_sem=recv,
            device_id=device, device_id_type=MESH,
        )

    def flip(bit, by):
        return bit + by - 2 * bit * by

    def aligned(value, by):
        return pl.multiple_of(value, by)

    def each_chip(run, near_first=False, halves=(0, 1), quarters=(0, 1)):
        turn = (lambda i: i) if near_first else (lambda i: 1 - i)

        @pl.loop(halves[0], halves[-1] + 1)
        def _(a):
            rb = flip(bits[0], turn(a))

            @pl.loop(quarters[0], quarters[-1] + 1)
            def _(b):
                l2 = flip(bits[1], turn(b))

                @pl.loop(0, 2)
                def _(c):
                    lb = l2 * 2 + flip(bits[2], turn(c))
                    run(rb * 4 + lb, rb, lb)

    peer = dev(chip, other)

    mine = pl.ds(2 * core, 2)
    theirs = pl.ds(2 * other, 2)
    half = pl.ds(aligned(16 * core, 16), 16)
    other_half = pl.ds(aligned(16 * other, 16), 16)
    loads = [
        pltpu.make_async_copy(cons, qo, loc_sem.at[0]),
        pltpu.make_async_copy(phase, po, loc_sem.at[1]),
        pltpu.make_async_copy(diag.at[:, :, :, other_half], do, loc_sem.at[2]),
        pltpu.make_async_copy(diag.at[:, :, :, half], dv.at[:, :, mine], loc_sem.at[3]),
        pltpu.make_async_copy(
            cons.at[:, :, pl.ds(aligned(8 * core, 8), 24)],
            qp.at[:, mine, pl.ds(aligned(8 * other, 8), 24)], loc_sem.at[4]),
        pltpu.make_async_copy(
            phase.at[:, pl.ds(aligned(8 * core, 8), 24)],
            pp.at[mine, pl.ds(aligned(8 * other, 8), 24)], loc_sem.at[5]),
    ]
    for copy in loads:
        copy.start()

    barrier = pltpu.get_barrier_semaphore()

    def greet(device):
        pl.semaphore_signal(barrier, inc=1, device_id=device, device_id_type=MESH)

    span_near = core * span_up + other * span_down
    span_far = core * span_down + other * span_up
    greet(dev(chip, core, span_near))
    greet(dev(chip, other, span_near))
    greet(dev(chip, core, span_far))
    for k in range(7, -1, -1):
        at = [flip(bits[n], (k >> (2 - n)) & 1) for n in range(3)]
        to = at[0] * 4 + at[1] * 2 + at[2]
        greet(dev(to, other))
        if k:
            greet(dev(to, core))

    loads[0].wait()
    loads[1].wait()
    for side, at in ((0, 31), (1, 0)):
        for ch in range(5):
            for plane in range(2):
                row_out[side, pl.ds(ch * 2 + plane, 1), :] = qo[ch, plane, pl.ds(at, 1), :]
        for plane in range(2):
            row_out[side, pl.ds(10 + plane, 1), :] = po[plane, pl.ds(at, 1), :].astype(f32)
        row_out[side, pl.ds(12, 4), :] = jnp.zeros((4, 512), f32)

    @pl.loop(0, 2)
    def _(plane):
        @pl.loop(0, 4)
        def _(part):
            rows = pl.ds(aligned(part * 8, 8), 8)
            fields = primitives([qo[ch, plane, rows, :] for ch in range(5)], po[plane, rows, :])
            wo[plane, rows, :] = 0.5 * (jnp.abs(fields[1]) + fields[6])

    def weighted(mat, w):
        return [[mat(i, j) * w for j in range(5)] for i in range(5)]

    def product(mat, right, w=None):
        cols = [matvec(mat, [right[i][j] for i in range(5)]) for j in range(5)]
        return [[cols[j][i] if w is None else cols[j][i] * w for j in range(5)] for i in range(5)]

    def put(ref, at, prod):
        for i in range(5):
            for j in range(5):
                ref[(*at, i, j)] = prod[i][j]

    def own_products(half_at, mat_of, m_at, n_at):
        def run(q, rb, lb):
            rows = pl.ds(aligned(rb * 8, 8), 8)
            lanes = pl.ds(aligned(lb * 128, 128), 128)
            w_rows = pl.ds(aligned(half_at * 16 + rb * 8, 8), 8)
            w = [wo[plane, w_rows, lanes] for plane in range(2)]
            mats = [
                (lambda i, j, plane=plane: mat_of(i, j, plane, rows, lanes)) for plane in range(2)
            ]
            put(m_at[0], (*m_at[1], q), product(mats[1], weighted(mats[0], w[0]), w[1]))
            put(n_at[0], (*n_at[1], q), product(mats[0], weighted(mats[1], w[1]), w[0]))

        each_chip(run)

    loads[2].wait()
    own_products(other, lambda i, j, p, r, l: do[i, j, p, r, l], (mx, ()), (nx, ()))
    loads[3].wait()
    own_products(core, lambda i, j, p, r, l: dv[i, j, 2 * core + p, r, l], (pm, (core,)), (pn, (core,)))
    loads[4].wait()
    loads[5].wait()

    pl.semaphore_wait(barrier, 18)

    ahead = chip + 2 * core - 1

    def halo(core_at, part):
        rb = flip(bits[0], 1 - part)
        src = pl.ds(aligned(16 * core_at + 8 * rb, 8), 8)
        dst = pl.ds(aligned(8 * rb, 8), 8)
        return [
            remote(qo.at[:, core, src], qg.at[other, :, dst], halo_send.at[0],
                   halo_recv.at[other, rb, 0], dev(ahead, core_at)),
            remote(po.at[core, src], pg.at[other, dst], halo_send.at[1],
                   halo_recv.at[other, rb, 1], dev(ahead, core_at)),
        ]

    sends_halo = jnp.logical_or(
        jnp.logical_and(core == 0, chip > 0), jnp.logical_and(core == 1, chip < CHIPS - 1)
    )


    peer_rows = pl.ds(aligned(8 * other, 8), 24)
    peer_dst = pl.ds(aligned(8 * core, 8), 24)
    swaps = [
        remote(qo.at[:, :, peer_rows], qp.at[:, mine, peer_dst], chip_send.at[0], chip_recv.at[0], peer),
        remote(po.at[:, peer_rows], pp.at[mine, peer_dst], chip_send.at[1], chip_recv.at[1], peer),
        remote(do, dv.at[:, :, mine], chip_send.at[2], chip_recv.at[2], peer),
    ]
    row_copies = [
        remote(row_out.at[0], row_in.at[core], row_send.at[0], row_recv.at[core], dev(chip, 0, span_up)),
        remote(row_out.at[1], row_in.at[core], row_send.at[1], row_recv.at[core], dev(chip, 1, span_down)),
    ]

    def mx_copy(q):
        return remote(mx.at[q], pm.at[core, q], mx_send, mx_recv.at[q], peer)

    def nx_copy():
        return remote(nx, pn.at[core], nx_send, nx_recv.at[0], peer)

    for copy in row_copies:
        copy.start()

    @pl.when(sends_halo)
    def _():
        for part in range(2):
            for core_at in range(2):
                for copy in halo(core_at, part):
                    copy.start()

    @pl.when(inner)
    def _():
        each_chip(lambda q, rb, lb: mx_copy(q).start())

    swaps[0].start()
    swaps[1].start()

    def slot(core_at, chip_at):
        return core_at * CHIPS + chip_at

    def to_solver(q, out, gathered, send, recv, when=None):
        to_self = jnp.logical_and(is_solver, q == chip)
        goes = jnp.logical_not(to_self)

        @pl.when(goes if when is None else jnp.logical_and(goes, when))
        def _():
            remote(out.at[q], gathered.at[slot(core, chip)], send, recv.at[0], dev(q, SOLVER)).start()

        @pl.when(to_self)
        def _():
            gathered[slot(core, chip)] = out[q]

    def chip_product(parts, left, right, out, q):
        mat = lambda i, j: parts[left, q, i, j]
        right_mat = [[parts[right, q, i, j] for j in range(5)] for i in range(5)]
        put(out, (q,), product(mat, right_mat))

    @pl.when(inner)
    def _():
        def run(q, rb, lb):
            mx_copy(q).wait_recv()
            chip_product(pm, 1, 0, m_out, q)
            to_solver(q, m_out, m_all, m_send, m_recv)

        each_chip(run)
        nx_copy().start()

    swaps[2].start()

    def send_n(half_at, quarters=(0, 1)):
        def run(q, rb, lb):
            chip_product(pn, 0, 1, n_out, q)
            to_solver(q, n_out, n_all, n_send, n_recv)

        @pl.when(inner)
        def _():
            each_chip(run, halves=(half_at,), quarters=quarters)

    def set_primitives(plane, first):
        rows = pl.ds(aligned(first, 8), 8)
        fields = primitives([qp[ch, plane, rows, :] for ch in range(5)], pp[plane, rows, :])
        for ch in range(7):
            prim[ch, plane + 1, rows, :] = fields[ch]
        prim[7, plane + 1, rows, :] = 0.5 * (jnp.abs(fields[1]) + fields[6])

    swaps[0].wait_recv()
    swaps[1].wait_recv()

    @pl.loop(0, 4)
    def _(plane):
        @pl.loop(0, 3)
        def _(part):
            set_primitives(plane, 8 * (other + part))

    lane = lax.broadcasted_iota(jnp.int32, (8, 512), 1)

    @pl.loop(0, 4)
    def _(plane):
        @pl.loop(0, 2)
        def _(part):
            rows = pl.ds(aligned(part * 8 + 8, 8), 8)
            out_rows = pl.ds(aligned(part * 8, 8), 8)
            cell = [prim[ch, plane + 1, rows, :] for ch in range(7)]
            below = []
            for ch in range(7):
                first = -cell[ch] if ch == 3 else cell[ch]
                below.append(jnp.where(lane == 0, first, pltpu.roll(cell[ch], 1, axis=1)))
            low = hllc(below, cell, 3)
            mass = cell[0] * cell[3]
            top = [
                mass, cell[1] * mass, cell[2] * mass, cell[3] * mass + cell[5],
                cell[4] * mass + cell[5] * cell[3],
            ]
            for ch in range(5):
                high = jnp.where(lane == 511, top[ch], pltpu.roll(low[ch], 511, axis=1))
                acc[ch, plane, out_rows, :] = high - low[ch]

    @pl.loop(0, 2)
    def _(part):
        rows = pl.ds(aligned(part * 8 + 8, 8), 8)
        out_rows = pl.ds(aligned(part * 8, 8), 8)

        @pl.loop(0, 3)
        def _(plane):
            states = lambda p: [prim[ch, p, rows, :] for ch in range(7)]
            face = hllc(states(plane + 1), states(plane + 2), 1)
            for ch in range(5):
                acc[ch, plane, out_rows, :] = acc[ch, plane, out_rows, :] + face[ch]
                acc[ch, plane + 1, out_rows, :] = acc[ch, plane + 1, out_rows, :] - face[ch]

    for core_at in range(2):
        remote(row_out.at[0], row_in.at[core_at], row_send.at[0], row_recv.at[core_at], peer).wait_recv()
    ghost_row = 7 + 17 * core
    for core_at in range(2):
        for plane in range(2):
            for ch in range(5):
                qp[ch, 2 * core_at + plane, pl.ds(ghost_row, 1), :] = row_in[
                    core_at, pl.ds(ch * 2 + plane, 1), :
                ]
            pp[2 * core_at + plane, pl.ds(ghost_row, 1), :] = row_in[
                core_at, pl.ds(10 + plane, 1), :
            ].astype(jnp.int32)

    @pl.loop(0, 4)
    def _(plane):
        set_primitives(plane, 24 * core)

    @pl.loop(0, 4)
    def _(plane):
        @pl.loop(0, 4)
        def _(part):
            lanes = pl.ds(aligned(part * 128, 128), 128)
            down = [prim[ch, plane + 1, pl.ds(7, 24), lanes] for ch in range(7)]
            cell = [prim[ch, plane + 1, pl.ds(8, 24), lanes] for ch in range(7)]
            low = hllc(down, cell, 2)
            for ch in range(5):
                high = pltpu.roll(low[ch], 23, axis=0)
                acc[ch, plane, :, lanes] = acc[ch, plane, :, lanes] + (high - low[ch])[:16]

    def block(plane, rb, lb):
        rows = pl.ds(aligned(rb * 8, 8), 8)
        lanes = pl.ds(aligned(lb * 128, 128), 128)
        return lambda i, j: dv[i, j, plane, rows, lanes]

    def weight(plane, rb, lb):
        return prim[7, plane + 1, pl.ds(aligned(rb * 8 + 8, 8), 8), pl.ds(aligned(lb * 128, 128), 128)]

    def cells(ref, plane, rb, lb):
        rows = pl.ds(aligned(rb * 8, 8), 8)
        lanes = pl.ds(aligned(lb * 128, 128), 128)
        return [ref[ch, plane, rows, lanes] for ch in range(5)]

    def set_cells(ref, plane, rb, lb, values):
        rows = pl.ds(aligned(rb * 8, 8), 8)
        lanes = pl.ds(aligned(lb * 128, 128), 128)
        for ch in range(5):
            ref[ch, plane, rows, lanes] = values[ch]

    def edge_face(side, rb):
        rows = pl.ds(aligned(rb * 8 + 8, 8), 8)
        out_rows = pl.ds(aligned(rb * 8, 8), 8)
        inside = [prim[ch, 1 + 3 * side, rows, :] for ch in range(7)]

        def add(outside):
            face = hllc(outside, inside, 1) if side == 0 else hllc(inside, outside, 1)
            for ch in range(5):
                value = acc[ch, 3 * side, out_rows, :]
                acc[ch, 3 * side, out_rows, :] = value - face[ch] if side == 0 else value + face[ch]

        at_end = chip == (CHIPS - 1) * side

        @pl.when(at_end)
        def _():
            add(inside)

        @pl.when(jnp.logical_not(at_end))
        def _():
            dst = pl.ds(aligned(rb * 8, 8), 8)
            remote(qg.at[side, :, dst], qg.at[side, :, dst], halo_send.at[0],
                   halo_recv.at[side, rb, 0], peer).wait_recv()
            remote(pg.at[side, dst], pg.at[side, dst], halo_send.at[1],
                   halo_recv.at[side, rb, 1], peer).wait_recv()
            add(primitives([qg[side, ch, dst, :] for ch in range(5)], pg[side, dst, :]))

    swaps[2].wait_recv()

    for group in range(2):
        rb_at = flip(bits[0], 1 - group)
        for side in range(2):
            edge_face(side, rb_at)

        def local_forward(q, rb, lb):
            flow = None
            for plane in range(4):
                value = [face_area * x for x in cells(acc, plane, rb, lb)]
                set_cells(res, plane, rb, lb, value)
                entry = [-x for x in value] if flow is None else [y - x for x, y in zip(value, flow)]
                value = matvec(block(plane, rb, lb), entry)
                set_cells(swp, plane, rb, lb, value)
                w = weight(plane, rb, lb)
                flow = [w * x for x in value]
            for ch in range(5):
                g_out[q, ch] = flow[ch]
            to_solver(q, g_out, g_all, g_send, g_recv, chip < CHIPS - 1)

        each_chip(local_forward, halves=(group,))

    @pl.when(inner)
    def _():
        nx_copy().wait_recv()


    def response(q, rb, lb):
        blocks = [block(plane, rb, lb) for plane in range(4)]
        ws = [weight(plane, rb, lb) for plane in range(4)]

        def back(sweep):
            flow = [ws[3] * x for x in sweep[3]]
            for plane in (2, 1, 0):
                moved = matvec(blocks[plane], flow)
                flow = [ws[plane] * (x + y) for x, y in zip(sweep[plane], moved)]
            return flow

        local = back([cells(swp, plane, rb, lb) for plane in range(4)])
        for ch in range(5):
            hloc[q, ch] = local[ch]
        for j in range(5):
            sweep = [[blocks[0](i, j) for i in range(5)]]
            for plane in range(1, 4):
                sweep.append(matvec(blocks[plane], [ws[plane - 1] * x for x in sweep[-1]]))
            column = back(sweep)
            for i in range(5):
                km[q, i, j] = column[i]

    each_chip(response)

    def gather_wait(gathered, recv, total, fewer):
        @pl.when(fewer)
        def _():
            part = gathered.at[pl.ds(0, total - 1)]
            remote(part, part, sent.at[8], recv.at[0], peer).wait_recv()

        @pl.when(jnp.logical_not(fewer))
        def _():
            part = gathered.at[pl.ds(0, total)]
            remote(part, part, sent.at[8], recv.at[0], peer).wait_recv()

    def scatter(values, out, landed, send, recv, to_chip):
        for to_core in range(2):
            at = slot(to_core, to_chip)
            for ch in range(5):
                out[at, ch] = values[to_core][ch]

            def start():
                remote(out.at[at], landed.at[chip], send, recv.at[bits[0]], dev(to_chip, to_core)).start()

            if to_core == SOLVER:
                pl.when(chip != to_chip)(start)

                @pl.when(chip == to_chip)
                def _():
                    for ch in range(5):
                        landed[chip, ch] = values[to_core][ch]
            else:
                start()

    def recurrence(mats, vecs, out, landed, send, recv, order):
        flow = None
        for at, src in enumerate(order[:-1]):
            new = []
            for a in range(2):
                value = [vecs[slot(a, src), ch] for ch in range(5)]
                if at > 0:
                    moved = matvec(lambda i, j: mats[slot(a, src), i, j], flow[a])
                    value = [x + y for x, y in zip(value, moved)]
                new.append(value)
            flow = new
            scatter(flow, out, landed, send, recv, order[at + 1])

    @pl.when(is_solver)
    def _():
        gather_wait(m_all, m_recv, 2 * (CHIPS - 2), inner)
        gather_wait(g_all, g_recv, 2 * (CHIPS - 1), chip < CHIPS - 1)
        recurrence(m_all, g_all, f_out, f_all, f_send, f_recv, tuple(range(CHIPS)))
        send_n(0, (0,))
        send_n(0, (1,))
        send_n(1, (0,))
        send_n(1, (1,))

    @pl.when(jnp.logical_not(is_solver))
    def _():
        send_n(0, (0,))
        send_n(0, (1,))
        send_n(1, (0,))
        send_n(1, (1,))


    def landed_wait(landed, recv, rb):
        fewer = jnp.logical_and(is_solver, rb == bits[0])

        @pl.when(fewer)
        def _():
            part = landed.at[pl.ds(0, 3)]
            remote(part, part, sent.at[8], recv.at[rb], peer).wait_recv()

        @pl.when(jnp.logical_not(fewer))
        def _():
            part = landed.at[pl.ds(0, 4)]
            remote(part, part, sent.at[8], recv.at[rb], peer).wait_recv()

    @pl.when(chip == 0)
    def _():
        f_all[...] = jnp.zeros_like(f_all)

    def backward_start(q, rb, lb):
        moved = matvec(lambda i, j: km[q, i, j], [f_all[q, ch] for ch in range(5)])
        for ch in range(5):
            h_out[q, ch] = hloc[q, ch] + moved[ch]
        to_solver(q, h_out, h_all, h_send, h_recv, chip > 0)

    for group in range(2):
        @pl.when(chip > 0)
        def _():
            landed_wait(f_all, f_recv, flip(bits[0], group))

        each_chip(backward_start, near_first=True, halves=(group,))


    out_copies = [
        pltpu.make_async_copy(res.at[:, mine], resid.at[:, :, half], out_sem.at[0]),
        remote(res.at[:, theirs], resid.at[:, :, half], out_send.at[0], out_recv.at[0], peer),
    ]
    for copy in out_copies:
        copy.start()

    def both_sweeps(q, rb, lb):
        flow = [f_all[q, ch] for ch in range(5)]
        sweep = []
        for plane in range(4):
            entry = [y - x for x, y in zip(cells(res, plane, rb, lb), flow)]
            sweep.append(matvec(block(plane, rb, lb), entry))
            w = weight(plane, rb, lb)
            flow = [w * x for x in sweep[-1]]
        value = sweep[3]
        set_cells(swp, 3, rb, lb, value)
        for plane in (2, 1, 0):
            w = weight(plane + 1, rb, lb)
            moved = matvec(block(plane, rb, lb), [w * x for x in value])
            value = [x + y for x, y in zip(sweep[plane], moved)]
            set_cells(swp, plane, rb, lb, value)

    each_chip(both_sweeps)

    @pl.when(is_solver)
    def _():
        gather_wait(n_all, n_recv, 2 * (CHIPS - 2), inner)
        gather_wait(h_all, h_recv, 2 * (CHIPS - 1), chip > 0)
        recurrence(n_all, h_all, w_out, w_all, w_send, w_recv, tuple(range(CHIPS - 1, -1, -1)))

    @pl.when(chip == CHIPS - 1)
    def _():
        w_all[...] = jnp.zeros_like(w_all)

    def finish(q, rb, lb):
        flow = [w_all[q, ch] for ch in range(5)]
        for plane in (3, 2, 1, 0):
            moved = matvec(block(plane, rb, lb), flow)
            set_cells(upv, plane, rb, lb, [x + y for x, y in zip(cells(swp, plane, rb, lb), moved)])
            w = weight(plane, rb, lb)
            flow = [w * x for x in moved]

    def final(group):
        rb = flip(bits[0], group)
        src = pl.ds(aligned(8 * rb, 8), 8)
        dst = pl.ds(aligned(16 * core + 8 * rb, 8), 8)
        return [
            remote(upv.at[:, theirs, src], upd.at[:, :, dst], out_send.at[1 + group],
                   out_recv.at[1 + group], peer),
            pltpu.make_async_copy(upv.at[:, mine, src], upd.at[:, :, dst], out_sem.at[1 + group]),
        ]

    for group in range(2):
        @pl.when(chip < CHIPS - 1)
        def _():
            landed_wait(w_all, w_recv, flip(bits[0], group))

        each_chip(finish, near_first=True, halves=(group,))
        for copy in final(group):
            copy.start()

    for copy in swaps:
        copy.wait_send()
    for copy in row_copies:
        copy.wait_send()

    def drain(part, send):
        remote(part, part, send, nx_recv.at[0], peer).wait_send()

    @pl.when(sends_halo)
    def _():
        drain(qo.at[:, 0], halo_send.at[0])
        drain(po.at[0], halo_send.at[1])

    def drain_either(out, send, total, fewer, when):
        for less in (False, True):
            case = fewer if less else jnp.logical_not(fewer)

            @pl.when(case if when is None else jnp.logical_and(case, when))
            def _():
                drain(out.at[pl.ds(0, total - less)], send)

    @pl.when(inner)
    def _():
        drain(mx, mx_send)
        drain(nx, nx_send)

    drain_either(m_out, m_send, CHIPS, is_solver, inner)
    drain_either(n_out, n_send, CHIPS, is_solver, inner)
    drain_either(g_out, g_send, CHIPS, is_solver, chip < CHIPS - 1)
    drain_either(h_out, h_send, CHIPS, is_solver, chip > 0)
    drain_either(f_out, f_send, 2 * (CHIPS - 1), chip > 0, is_solver)
    drain_either(w_out, w_send, 2 * (CHIPS - 1), chip < CHIPS - 1, is_solver)

    out_copies[0].wait()
    out_copies[1].wait()
    for group in range(2):
        for copy in final(group):
            copy.wait()


def hand_over(update, residual, update_out, residual_out, held, read, written):
    pairs = [(0, update, update_out), (1, residual, residual_out)]
    loads = [
        pltpu.make_async_copy(src.at[ch], held.at[n, ch], read.at[n, ch])
        for n, src, _ in pairs
        for ch in range(5)
    ]
    stores = [
        pltpu.make_async_copy(held.at[n, ch], dst.at[ch], written.at[n, ch])
        for n, _, dst in pairs
        for ch in range(5)
    ]
    for copy in loads:
        copy.start()
    for load, store in zip(loads, stores):
        load.wait()
        store.start()
    for copy in stores:
        copy.wait()


def body(cons, phase, diag):
    dma = pltpu.SemaphoreType.DMA
    vm = lambda *shape: pltpu.VMEM(shape, f32)
    vi = lambda *shape: pltpu.VMEM(shape, jnp.int32)
    vecs = lambda *lead: vm(*lead, CHIPS, 5, 8, 128)
    mats = lambda *lead: vm(*lead, CHIPS, 5, 5, 8, 128)
    vecs2, mats2 = vm(2 * CHIPS, 5, 8, 128), vm(2 * CHIPS, 5, 5, 8, 128)
    scratch = [
        vm(5, 2, 32, 512), vi(2, 32, 512), vm(5, 4, 32, 512), vi(4, 32, 512),
        vm(2, 5, 16, 512), vi(2, 16, 512), vm(2, 16, 512), vm(2, 16, 512), vm(2, 32, 512),
        vm(5, 5, 2, 16, 512), vm(5, 5, 4, 16, 512), vm(8, 5, 32, 512),
        vm(5, 4, 16, 512), vm(5, 4, 16, 512), vm(5, 4, 16, 512), vm(5, 4, 16, 512), vecs(),
        mats(), mats(), mats(2), mats(2), mats(), mats(), mats(), mats2, mats2,
        vecs(), vecs2, vecs2, vecs(), vecs(), vecs2, vecs2, vecs(),
        dma((6,)), dma((3,)), dma((3,)), dma((CHIPS,)), dma((2,)), dma((2, 2, 2)), dma((2,)), dma((2,)),
        dma((9,)), dma((1,)), dma((1,)), dma((1,)), dma((1,)), dma((1,)), dma((2,)), dma((2,)),
        dma((3,)), dma((3,)), dma((3,)),
    ]
    out = jax.ShapeDtypeStruct(cons.shape, f32)
    anywhere = pl.BlockSpec(memory_space=pl.ANY)
    hbm = pl.BlockSpec(memory_space=pltpu.HBM)
    update, residual = pl.pallas_call(
        kernel,
        out_shape=(out, out),
        in_specs=[hbm] * 3,
        out_specs=(anywhere, anywhere),
        scratch_shapes=scratch,
        compiler_params=pltpu.CompilerParams(
            collective_id=0, has_side_effects=True, vmem_limit_bytes=60 * 2**20
        ),
        name="flow_sweep",
    )(cons, phase, diag)
    return pl.pallas_call(
        hand_over,
        out_shape=(out, out),
        in_specs=[hbm] * 2,
        out_specs=(hbm, hbm),
        scratch_shapes=[vm(2, *cons.shape), dma((2, 5)), dma((2, 5))],
        name="hand_over",
    )(update, residual)

def solution(mesh):
    in_specs = (
        P(None, "stream", "span", None),
        P("stream", "span", None),
        P(None, None, "stream", "span", None),
    )
    out_specs = (P(None, "stream", "span", None), P(None, "stream", "span", None))
    return jax.shard_map(body, mesh=mesh, in_specs=in_specs, out_specs=out_specs, check_vma=False)
```

```python
import jax
import jax.numpy as jnp
from jax import lax
from jax.experimental import pallas as pl
from jax.experimental.pallas import tpu as pltpu
from jax.sharding import PartitionSpec as P

face_area = 0.0625
MESH = pl.DeviceIdType.MESH
CHIPS = 8
SOLVER = 1
f32 = jnp.float32


def eos(phase):
    ratio = jnp.where(phase == 0, 4.4, jnp.where(phase == 1, 1.4, 2.0)).astype(f32)
    stiff = jnp.where(phase == 0, 1.0, jnp.where(phase == 1, 0.0, 0.5)).astype(f32)
    return ratio, stiff


def primitives(cons, phase):
    ratio, stiff = eos(phase)
    density = cons[0]
    inverse = 1.0 / density
    u1, u2, u3 = cons[1] * inverse, cons[2] * inverse, cons[3] * inverse
    kinetic = 0.5 * density * (u1 * u1 + u2 * u2 + u3 * u3)
    pressure = (ratio - 1.0) * (cons[4] - kinetic) - ratio * stiff
    sound = jnp.sqrt(ratio * (pressure + stiff) * inverse)
    return [density, u1, u2, u3, cons[4] * inverse, pressure, sound]


def hllc(left, right, normal):
    ql, qr = left[normal], right[normal]
    cl, cr = left[6], right[6]
    sl = jnp.minimum(ql - cl, qr - cr)
    sr = jnp.maximum(ql + cl, qr + cr)
    ml = left[0] * (sl - ql)
    mr = right[0] * (sr - qr)
    contact = (right[5] - left[5] + ml * ql - mr * qr) / (ml - mr)
    supersonic = sl >= 0.0
    ahead = contact >= 0.0
    use_left = jnp.logical_or(supersonic, ahead)
    starred = jnp.logical_and(
        jnp.logical_not(supersonic), jnp.logical_or(ahead, sr >= 0.0)
    )
    pick = lambda a, b: jnp.where(use_left, a, b)
    s, m, q = pick(sl, sr), pick(ml, mr), pick(ql, qr)
    p, e = pick(left[5], right[5]), pick(left[4], right[4])
    ss = jnp.where(starred, contact, q)
    inv = 1.0 / (s - ss)
    mass = m * inv * ss
    out = [mass]
    for d in (1, 2, 3):
        if d == normal:
            out.append(s * mass - q * m + p)
        else:
            out.append(pick(left[d], right[d]) * mass)
    out.append(p * q + e * mass + s * (ss - q) * (mass + p * inv))
    return out


def matvec(mat, vec):
    return [
        mat(i, 0) * vec[0]
        + mat(i, 1) * vec[1]
        + mat(i, 2) * vec[2]
        + mat(i, 3) * vec[3]
        + mat(i, 4) * vec[4]
        for i in range(5)
    ]


def kernel(
    cons, phase, diag, upd, resid,
    qo, po, qp, pp, qg, pg, row_out, row_in, wo, do, dv, prim, acc, swp, res, upv, hloc,
    mx, nx, pm, pn, km, m_out, n_out, m_all, n_all,
    g_out, g_all, f_out, f_all, h_out, h_all, w_out, w_all,
    loc_sem, chip_send, chip_recv, mx_recv, halo_send, halo_recv, row_send, row_recv,
    sent, nx_recv, m_recv, n_recv, g_recv, h_recv, f_recv, w_recv, out_sem, out_send, out_recv,
):
    stream = lax.axis_index("stream")
    span = lax.axis_index("span")
    spans = lax.axis_size("span")
    core = stream % 2
    chip = stream // 2
    other = 1 - core
    bits = (chip // 4, (chip // 2) % 2, chip % 2)
    span_up = (span + 1) % spans
    span_down = (span + spans - 1) % spans
    is_solver = core == SOLVER
    mx_send, nx_send, m_send, n_send, g_send, h_send, f_send, w_send = [sent.at[k] for k in range(8)]
    inner = jnp.logical_and(chip > 0, chip < CHIPS - 1)

    def dev(chip_at, core_at, span_at=None):
        return {
            "stream": chip_at * 2 + core_at,
            "span": span if span_at is None else span_at,
        }

    def remote(src, dst, send, recv, device):
        return pltpu.make_async_remote_copy(
            src_ref=src, dst_ref=dst, send_sem=send, recv_sem=recv,
            device_id=device, device_id_type=MESH,
        )

    def flip(bit, by):
        return bit + by - 2 * bit * by

    def aligned(value, by):
        return pl.multiple_of(value, by)

    def each_chip(run, near_first=False, halves=(0, 1), quarters=(0, 1)):
        turn = (lambda i: i) if near_first else (lambda i: 1 - i)

        @pl.loop(halves[0], halves[-1] + 1)
        def _(a):
            rb = flip(bits[0], turn(a))

            @pl.loop(quarters[0], quarters[-1] + 1)
            def _(b):
                l2 = flip(bits[1], turn(b))

                @pl.loop(0, 2)
                def _(c):
                    lb = l2 * 2 + flip(bits[2], turn(c))
                    run(rb * 4 + lb, rb, lb)

    peer = dev(chip, other)

    mine = pl.ds(2 * core, 2)
    theirs = pl.ds(2 * other, 2)
    half = pl.ds(aligned(16 * core, 16), 16)
    other_half = pl.ds(aligned(16 * other, 16), 16)
    loads = [
        pltpu.make_async_copy(cons, qo, loc_sem.at[0]),
        pltpu.make_async_copy(phase, po, loc_sem.at[1]),
        pltpu.make_async_copy(diag.at[:, :, :, other_half], do, loc_sem.at[2]),
        pltpu.make_async_copy(diag.at[:, :, :, half], dv.at[:, :, mine], loc_sem.at[3]),
        pltpu.make_async_copy(
            cons.at[:, :, pl.ds(aligned(8 * core, 8), 24)],
            qp.at[:, mine, pl.ds(aligned(8 * other, 8), 24)], loc_sem.at[4]),
        pltpu.make_async_copy(
            phase.at[:, pl.ds(aligned(8 * core, 8), 24)],
            pp.at[mine, pl.ds(aligned(8 * other, 8), 24)], loc_sem.at[5]),
    ]
    for copy in loads:
        copy.start()

    barrier = pltpu.get_barrier_semaphore()

    def greet(device):
        pl.semaphore_signal(barrier, inc=1, device_id=device, device_id_type=MESH)

    span_near = core * span_up + other * span_down
    span_far = core * span_down + other * span_up
    greet(dev(chip, core, span_near))
    greet(dev(chip, other, span_near))
    greet(dev(chip, core, span_far))
    for k in range(7, -1, -1):
        at = [flip(bits[n], (k >> (2 - n)) & 1) for n in range(3)]
        to = at[0] * 4 + at[1] * 2 + at[2]
        greet(dev(to, other))
        if k:
            greet(dev(to, core))

    loads[0].wait()
    loads[1].wait()
    for side, at in ((0, 31), (1, 0)):
        for ch in range(5):
            for plane in range(2):
                row_out[side, pl.ds(ch * 2 + plane, 1), :] = qo[ch, plane, pl.ds(at, 1), :]
        for plane in range(2):
            row_out[side, pl.ds(10 + plane, 1), :] = po[plane, pl.ds(at, 1), :].astype(f32)
        row_out[side, pl.ds(12, 4), :] = jnp.zeros((4, 512), f32)

    @pl.loop(0, 2)
    def _(plane):
        @pl.loop(0, 4)
        def _(part):
            rows = pl.ds(aligned(part * 8, 8), 8)
            fields = primitives([qo[ch, plane, rows, :] for ch in range(5)], po[plane, rows, :])
            wo[plane, rows, :] = 0.5 * (jnp.abs(fields[1]) + fields[6])

    def weighted(mat, w):
        return [[mat(i, j) * w for j in range(5)] for i in range(5)]

    def product(mat, right, w=None):
        cols = [matvec(mat, [right[i][j] for i in range(5)]) for j in range(5)]
        return [[cols[j][i] if w is None else cols[j][i] * w for j in range(5)] for i in range(5)]

    def put(ref, at, prod):
        for i in range(5):
            for j in range(5):
                ref[(*at, i, j)] = prod[i][j]

    def own_products(half_at, mat_of, m_at, n_at):
        def run(q, rb, lb):
            rows = pl.ds(aligned(rb * 8, 8), 8)
            lanes = pl.ds(aligned(lb * 128, 128), 128)
            w_rows = pl.ds(aligned(half_at * 16 + rb * 8, 8), 8)
            w = [wo[plane, w_rows, lanes] for plane in range(2)]
            mats = [
                (lambda i, j, plane=plane: mat_of(i, j, plane, rows, lanes)) for plane in range(2)
            ]
            put(m_at[0], (*m_at[1], q), product(mats[1], weighted(mats[0], w[0]), w[1]))
            put(n_at[0], (*n_at[1], q), product(mats[0], weighted(mats[1], w[1]), w[0]))

        each_chip(run)

    loads[2].wait()
    own_products(other, lambda i, j, p, r, l: do[i, j, p, r, l], (mx, ()), (nx, ()))
    loads[3].wait()
    own_products(core, lambda i, j, p, r, l: dv[i, j, 2 * core + p, r, l], (pm, (core,)), (pn, (core,)))
    loads[4].wait()
    loads[5].wait()

    pl.semaphore_wait(barrier, 18)

    ahead = chip + 2 * core - 1

    def halo(core_at, part):
        rb = flip(bits[0], 1 - part)
        src = pl.ds(aligned(16 * core_at + 8 * rb, 8), 8)
        dst = pl.ds(aligned(8 * rb, 8), 8)
        return [
            remote(qo.at[:, core, src], qg.at[other, :, dst], halo_send.at[0],
                   halo_recv.at[other, rb, 0], dev(ahead, core_at)),
            remote(po.at[core, src], pg.at[other, dst], halo_send.at[1],
                   halo_recv.at[other, rb, 1], dev(ahead, core_at)),
        ]

    sends_halo = jnp.logical_or(
        jnp.logical_and(core == 0, chip > 0), jnp.logical_and(core == 1, chip < CHIPS - 1)
    )


    peer_rows = pl.ds(aligned(8 * other, 8), 24)
    peer_dst = pl.ds(aligned(8 * core, 8), 24)
    swaps = [
        remote(qo.at[:, :, peer_rows], qp.at[:, mine, peer_dst], chip_send.at[0], chip_recv.at[0], peer),
        remote(po.at[:, peer_rows], pp.at[mine, peer_dst], chip_send.at[1], chip_recv.at[1], peer),
        remote(do, dv.at[:, :, mine], chip_send.at[2], chip_recv.at[2], peer),
    ]
    row_copies = [
        remote(row_out.at[0], row_in.at[core], row_send.at[0], row_recv.at[core], dev(chip, 0, span_up)),
        remote(row_out.at[1], row_in.at[core], row_send.at[1], row_recv.at[core], dev(chip, 1, span_down)),
    ]

    def mx_copy(q):
        return remote(mx.at[q], pm.at[core, q], mx_send, mx_recv.at[q], peer)

    def nx_copy():
        return remote(nx, pn.at[core], nx_send, nx_recv.at[0], peer)

    for copy in row_copies:
        copy.start()

    @pl.when(sends_halo)
    def _():
        for part in range(2):
            for core_at in range(2):
                for copy in halo(core_at, part):
                    copy.start()

    @pl.when(inner)
    def _():
        each_chip(lambda q, rb, lb: mx_copy(q).start())

    swaps[0].start()
    swaps[1].start()

    def slot(core_at, chip_at):
        return core_at * CHIPS + chip_at

    def to_solver(q, out, gathered, send, recv, when=None):
        to_self = jnp.logical_and(is_solver, q == chip)
        goes = jnp.logical_not(to_self)

        @pl.when(goes if when is None else jnp.logical_and(goes, when))
        def _():
            remote(out.at[q], gathered.at[slot(core, chip)], send, recv.at[0], dev(q, SOLVER)).start()

        @pl.when(to_self)
        def _():
            gathered[slot(core, chip)] = out[q]

    def chip_product(parts, left, right, out, q):
        mat = lambda i, j: parts[left, q, i, j]
        right_mat = [[parts[right, q, i, j] for j in range(5)] for i in range(5)]
        put(out, (q,), product(mat, right_mat))

    @pl.when(inner)
    def _():
        def run(q, rb, lb):
            mx_copy(q).wait_recv()
            chip_product(pm, 1, 0, m_out, q)
            to_solver(q, m_out, m_all, m_send, m_recv)

        each_chip(run)
        nx_copy().start()

    swaps[2].start()

    def send_n():
        @pl.when(inner)
        def _():
            each_chip(lambda q, rb, lb: to_solver(q, n_out, n_all, n_send, n_recv))

    def set_primitives(plane, first):
        rows = pl.ds(aligned(first, 8), 8)
        fields = primitives([qp[ch, plane, rows, :] for ch in range(5)], pp[plane, rows, :])
        for ch in range(7):
            prim[ch, plane + 1, rows, :] = fields[ch]
        prim[7, plane + 1, rows, :] = 0.5 * (jnp.abs(fields[1]) + fields[6])

    swaps[0].wait_recv()
    swaps[1].wait_recv()

    @pl.loop(0, 4)
    def _(plane):
        @pl.loop(0, 3)
        def _(part):
            set_primitives(plane, 8 * (other + part))

    lane = lax.broadcasted_iota(jnp.int32, (8, 512), 1)

    @pl.loop(0, 4)
    def _(plane):
        @pl.loop(0, 2)
        def _(part):
            rows = pl.ds(aligned(part * 8 + 8, 8), 8)
            out_rows = pl.ds(aligned(part * 8, 8), 8)
            cell = [prim[ch, plane + 1, rows, :] for ch in range(7)]
            below = []
            for ch in range(7):
                first = -cell[ch] if ch == 3 else cell[ch]
                below.append(jnp.where(lane == 0, first, pltpu.roll(cell[ch], 1, axis=1)))
            low = hllc(below, cell, 3)
            mass = cell[0] * cell[3]
            top = [
                mass, cell[1] * mass, cell[2] * mass, cell[3] * mass + cell[5],
                cell[4] * mass + cell[5] * cell[3],
            ]
            for ch in range(5):
                high = jnp.where(lane == 511, top[ch], pltpu.roll(low[ch], 511, axis=1))
                acc[ch, plane, out_rows, :] = high - low[ch]

    @pl.loop(0, 2)
    def _(part):
        rows = pl.ds(aligned(part * 8 + 8, 8), 8)
        out_rows = pl.ds(aligned(part * 8, 8), 8)

        @pl.loop(0, 3)
        def _(plane):
            states = lambda p: [prim[ch, p, rows, :] for ch in range(7)]
            face = hllc(states(plane + 1), states(plane + 2), 1)
            for ch in range(5):
                acc[ch, plane, out_rows, :] = acc[ch, plane, out_rows, :] + face[ch]
                acc[ch, plane + 1, out_rows, :] = acc[ch, plane + 1, out_rows, :] - face[ch]

    for core_at in range(2):
        remote(row_out.at[0], row_in.at[core_at], row_send.at[0], row_recv.at[core_at], peer).wait_recv()
    ghost_row = 7 + 17 * core
    for core_at in range(2):
        for plane in range(2):
            for ch in range(5):
                qp[ch, 2 * core_at + plane, pl.ds(ghost_row, 1), :] = row_in[
                    core_at, pl.ds(ch * 2 + plane, 1), :
                ]
            pp[2 * core_at + plane, pl.ds(ghost_row, 1), :] = row_in[
                core_at, pl.ds(10 + plane, 1), :
            ].astype(jnp.int32)

    @pl.loop(0, 4)
    def _(plane):
        set_primitives(plane, 24 * core)

    @pl.loop(0, 4)
    def _(plane):
        @pl.loop(0, 4)
        def _(part):
            lanes = pl.ds(aligned(part * 128, 128), 128)
            down = [prim[ch, plane + 1, pl.ds(7, 24), lanes] for ch in range(7)]
            cell = [prim[ch, plane + 1, pl.ds(8, 24), lanes] for ch in range(7)]
            low = hllc(down, cell, 2)
            for ch in range(5):
                high = pltpu.roll(low[ch], 23, axis=0)
                acc[ch, plane, :, lanes] = acc[ch, plane, :, lanes] + (high - low[ch])[:16]

    def block(plane, rb, lb):
        rows = pl.ds(aligned(rb * 8, 8), 8)
        lanes = pl.ds(aligned(lb * 128, 128), 128)
        return lambda i, j: dv[i, j, plane, rows, lanes]

    def weight(plane, rb, lb):
        return prim[7, plane + 1, pl.ds(aligned(rb * 8 + 8, 8), 8), pl.ds(aligned(lb * 128, 128), 128)]

    def cells(ref, plane, rb, lb):
        rows = pl.ds(aligned(rb * 8, 8), 8)
        lanes = pl.ds(aligned(lb * 128, 128), 128)
        return [ref[ch, plane, rows, lanes] for ch in range(5)]

    def set_cells(ref, plane, rb, lb, values):
        rows = pl.ds(aligned(rb * 8, 8), 8)
        lanes = pl.ds(aligned(lb * 128, 128), 128)
        for ch in range(5):
            ref[ch, plane, rows, lanes] = values[ch]

    def edge_face(side, rb):
        rows = pl.ds(aligned(rb * 8 + 8, 8), 8)
        out_rows = pl.ds(aligned(rb * 8, 8), 8)
        inside = [prim[ch, 1 + 3 * side, rows, :] for ch in range(7)]

        def add(outside):
            face = hllc(outside, inside, 1) if side == 0 else hllc(inside, outside, 1)
            for ch in range(5):
                value = acc[ch, 3 * side, out_rows, :]
                acc[ch, 3 * side, out_rows, :] = value - face[ch] if side == 0 else value + face[ch]

        at_end = chip == (CHIPS - 1) * side

        @pl.when(at_end)
        def _():
            add(inside)

        @pl.when(jnp.logical_not(at_end))
        def _():
            dst = pl.ds(aligned(rb * 8, 8), 8)
            remote(qg.at[side, :, dst], qg.at[side, :, dst], halo_send.at[0],
                   halo_recv.at[side, rb, 0], peer).wait_recv()
            remote(pg.at[side, dst], pg.at[side, dst], halo_send.at[1],
                   halo_recv.at[side, rb, 1], peer).wait_recv()
            add(primitives([qg[side, ch, dst, :] for ch in range(5)], pg[side, dst, :]))

    swaps[2].wait_recv()

    for group in range(2):
        rb_at = flip(bits[0], 1 - group)
        for side in range(2):
            edge_face(side, rb_at)

        def local_forward(q, rb, lb):
            flow = None
            for plane in range(4):
                value = [face_area * x for x in cells(acc, plane, rb, lb)]
                set_cells(res, plane, rb, lb, value)
                entry = [-x for x in value] if flow is None else [y - x for x, y in zip(value, flow)]
                value = matvec(block(plane, rb, lb), entry)
                set_cells(swp, plane, rb, lb, value)
                w = weight(plane, rb, lb)
                flow = [w * x for x in value]
            for ch in range(5):
                g_out[q, ch] = flow[ch]
            to_solver(q, g_out, g_all, g_send, g_recv, chip < CHIPS - 1)

        each_chip(local_forward, halves=(group,))

    @pl.when(inner)
    def _():
        nx_copy().wait_recv()
        each_chip(lambda q, rb, lb: chip_product(pn, 0, 1, n_out, q))


    def response(q, rb, lb):
        blocks = [block(plane, rb, lb) for plane in range(4)]
        ws = [weight(plane, rb, lb) for plane in range(4)]

        def back(sweep):
            flow = [ws[3] * x for x in sweep[3]]
            for plane in (2, 1, 0):
                moved = matvec(blocks[plane], flow)
                flow = [ws[plane] * (x + y) for x, y in zip(sweep[plane], moved)]
            return flow

        local = back([cells(swp, plane, rb, lb) for plane in range(4)])
        for ch in range(5):
            hloc[q, ch] = local[ch]
        for j in range(5):
            sweep = [[blocks[0](i, j) for i in range(5)]]
            for plane in range(1, 4):
                sweep.append(matvec(blocks[plane], [ws[plane - 1] * x for x in sweep[-1]]))
            column = back(sweep)
            for i in range(5):
                km[q, i, j] = column[i]

    each_chip(response)

    def gather_wait(gathered, recv, total, fewer):
        @pl.when(fewer)
        def _():
            part = gathered.at[pl.ds(0, total - 1)]
            remote(part, part, sent.at[8], recv.at[0], peer).wait_recv()

        @pl.when(jnp.logical_not(fewer))
        def _():
            part = gathered.at[pl.ds(0, total)]
            remote(part, part, sent.at[8], recv.at[0], peer).wait_recv()

    def scatter(values, out, landed, send, recv, to_chip):
        for to_core in range(2):
            at = slot(to_core, to_chip)
            for ch in range(5):
                out[at, ch] = values[to_core][ch]

            def start():
                remote(out.at[at], landed.at[chip], send, recv.at[bits[0]], dev(to_chip, to_core)).start()

            if to_core == SOLVER:
                pl.when(chip != to_chip)(start)

                @pl.when(chip == to_chip)
                def _():
                    for ch in range(5):
                        landed[chip, ch] = values[to_core][ch]
            else:
                start()

    def recurrence(mats, vecs, out, landed, send, recv, order):
        flow = None
        for at, src in enumerate(order[:-1]):
            new = []
            for a in range(2):
                value = [vecs[slot(a, src), ch] for ch in range(5)]
                if at > 0:
                    moved = matvec(lambda i, j: mats[slot(a, src), i, j], flow[a])
                    value = [x + y for x, y in zip(value, moved)]
                new.append(value)
            flow = new
            scatter(flow, out, landed, send, recv, order[at + 1])

    @pl.when(is_solver)
    def _():
        gather_wait(m_all, m_recv, 2 * (CHIPS - 2), inner)
        gather_wait(g_all, g_recv, 2 * (CHIPS - 1), chip < CHIPS - 1)
        recurrence(m_all, g_all, f_out, f_all, f_send, f_recv, tuple(range(CHIPS)))
        send_n()

    @pl.when(jnp.logical_not(is_solver))
    def _():
        send_n()


    def landed_wait(landed, recv, rb):
        fewer = jnp.logical_and(is_solver, rb == bits[0])

        @pl.when(fewer)
        def _():
            part = landed.at[pl.ds(0, 3)]
            remote(part, part, sent.at[8], recv.at[rb], peer).wait_recv()

        @pl.when(jnp.logical_not(fewer))
        def _():
            part = landed.at[pl.ds(0, 4)]
            remote(part, part, sent.at[8], recv.at[rb], peer).wait_recv()

    @pl.when(chip == 0)
    def _():
        f_all[...] = jnp.zeros_like(f_all)

    def backward_start(q, rb, lb):
        moved = matvec(lambda i, j: km[q, i, j], [f_all[q, ch] for ch in range(5)])
        for ch in range(5):
            h_out[q, ch] = hloc[q, ch] + moved[ch]
        to_solver(q, h_out, h_all, h_send, h_recv, chip > 0)

    for group in range(2):
        @pl.when(chip > 0)
        def _():
            landed_wait(f_all, f_recv, flip(bits[0], group))

        each_chip(backward_start, near_first=True, halves=(group,))


    def both_sweeps(q, rb, lb):
        flow = [f_all[q, ch] for ch in range(5)]
        sweep = []
        for plane in range(4):
            entry = [y - x for x, y in zip(cells(res, plane, rb, lb), flow)]
            sweep.append(matvec(block(plane, rb, lb), entry))
            w = weight(plane, rb, lb)
            flow = [w * x for x in sweep[-1]]
        value = sweep[3]
        set_cells(swp, 3, rb, lb, value)
        for plane in (2, 1, 0):
            w = weight(plane + 1, rb, lb)
            moved = matvec(block(plane, rb, lb), [w * x for x in value])
            value = [x + y for x, y in zip(sweep[plane], moved)]
            set_cells(swp, plane, rb, lb, value)

    each_chip(both_sweeps)

    @pl.when(is_solver)
    def _():
        gather_wait(n_all, n_recv, 2 * (CHIPS - 2), inner)
        gather_wait(h_all, h_recv, 2 * (CHIPS - 1), chip > 0)
        recurrence(n_all, h_all, w_out, w_all, w_send, w_recv, tuple(range(CHIPS - 1, -1, -1)))

    out_copies = [
        pltpu.make_async_copy(res.at[:, mine], resid.at[:, :, half], out_sem.at[0]),
        remote(res.at[:, theirs], resid.at[:, :, half], out_send.at[0], out_recv.at[0], peer),
    ]
    for copy in out_copies:
        copy.start()

    @pl.when(chip == CHIPS - 1)
    def _():
        w_all[...] = jnp.zeros_like(w_all)

    def finish(q, rb, lb):
        flow = [w_all[q, ch] for ch in range(5)]
        for plane in (3, 2, 1, 0):
            moved = matvec(block(plane, rb, lb), flow)
            set_cells(upv, plane, rb, lb, [x + y for x, y in zip(cells(swp, plane, rb, lb), moved)])
            w = weight(plane, rb, lb)
            flow = [w * x for x in moved]

    def final(group):
        rb = flip(bits[0], group)
        src = pl.ds(aligned(8 * rb, 8), 8)
        dst = pl.ds(aligned(16 * core + 8 * rb, 8), 8)
        return [
            remote(upv.at[:, theirs, src], upd.at[:, :, dst], out_send.at[1 + group],
                   out_recv.at[1 + group], peer),
            pltpu.make_async_copy(upv.at[:, mine, src], upd.at[:, :, dst], out_sem.at[1 + group]),
        ]

    for group in range(2):
        @pl.when(chip < CHIPS - 1)
        def _():
            landed_wait(w_all, w_recv, flip(bits[0], group))

        each_chip(finish, near_first=True, halves=(group,))
        for copy in final(group):
            copy.start()

    for copy in swaps:
        copy.wait_send()
    for copy in row_copies:
        copy.wait_send()

    def drain(part, send):
        remote(part, part, send, nx_recv.at[0], peer).wait_send()

    @pl.when(sends_halo)
    def _():
        drain(qo.at[:, 0], halo_send.at[0])
        drain(po.at[0], halo_send.at[1])

    def drain_either(out, send, total, fewer, when):
        for less in (False, True):
            case = fewer if less else jnp.logical_not(fewer)

            @pl.when(case if when is None else jnp.logical_and(case, when))
            def _():
                drain(out.at[pl.ds(0, total - less)], send)

    @pl.when(inner)
    def _():
        drain(mx, mx_send)
        drain(nx, nx_send)

    drain_either(m_out, m_send, CHIPS, is_solver, inner)
    drain_either(n_out, n_send, CHIPS, is_solver, inner)
    drain_either(g_out, g_send, CHIPS, is_solver, chip < CHIPS - 1)
    drain_either(h_out, h_send, CHIPS, is_solver, chip > 0)
    drain_either(f_out, f_send, 2 * (CHIPS - 1), chip > 0, is_solver)
    drain_either(w_out, w_send, 2 * (CHIPS - 1), chip < CHIPS - 1, is_solver)

    out_copies[0].wait()
    out_copies[1].wait()
    for group in range(2):
        for copy in final(group):
            copy.wait()


def hand_over(update, residual, update_out, residual_out, held, read, written):
    pairs = [(0, update, update_out), (1, residual, residual_out)]
    loads = [
        pltpu.make_async_copy(src.at[ch], held.at[n, ch], read.at[n, ch])
        for n, src, _ in pairs
        for ch in range(5)
    ]
    stores = [
        pltpu.make_async_copy(held.at[n, ch], dst.at[ch], written.at[n, ch])
        for n, _, dst in pairs
        for ch in range(5)
    ]
    for copy in loads:
        copy.start()
    for load, store in zip(loads, stores):
        load.wait()
        store.start()
    for copy in stores:
        copy.wait()


def body(cons, phase, diag):
    dma = pltpu.SemaphoreType.DMA
    vm = lambda *shape: pltpu.VMEM(shape, f32)
    vi = lambda *shape: pltpu.VMEM(shape, jnp.int32)
    vecs = lambda *lead: vm(*lead, CHIPS, 5, 8, 128)
    mats = lambda *lead: vm(*lead, CHIPS, 5, 5, 8, 128)
    vecs2, mats2 = vm(2 * CHIPS, 5, 8, 128), vm(2 * CHIPS, 5, 5, 8, 128)
    scratch = [
        vm(5, 2, 32, 512), vi(2, 32, 512), vm(5, 4, 32, 512), vi(4, 32, 512),
        vm(2, 5, 16, 512), vi(2, 16, 512), vm(2, 16, 512), vm(2, 16, 512), vm(2, 32, 512),
        vm(5, 5, 2, 16, 512), vm(5, 5, 4, 16, 512), vm(8, 5, 32, 512),
        vm(5, 4, 16, 512), vm(5, 4, 16, 512), vm(5, 4, 16, 512), vm(5, 4, 16, 512), vecs(),
        mats(), mats(), mats(2), mats(2), mats(), mats(), mats(), mats2, mats2,
        vecs(), vecs2, vecs2, vecs(), vecs(), vecs2, vecs2, vecs(),
        dma((6,)), dma((3,)), dma((3,)), dma((CHIPS,)), dma((2,)), dma((2, 2, 2)), dma((2,)), dma((2,)),
        dma((9,)), dma((1,)), dma((1,)), dma((1,)), dma((1,)), dma((1,)), dma((2,)), dma((2,)),
        dma((3,)), dma((3,)), dma((3,)),
    ]
    out = jax.ShapeDtypeStruct(cons.shape, f32)
    anywhere = pl.BlockSpec(memory_space=pl.ANY)
    hbm = pl.BlockSpec(memory_space=pltpu.HBM)
    update, residual = pl.pallas_call(
        kernel,
        out_shape=(out, out),
        in_specs=[hbm] * 3,
        out_specs=(anywhere, anywhere),
        scratch_shapes=scratch,
        compiler_params=pltpu.CompilerParams(
            collective_id=0, has_side_effects=True, vmem_limit_bytes=60 * 2**20
        ),
        name="flow_sweep",
    )(cons, phase, diag)
    return pl.pallas_call(
        hand_over,
        out_shape=(out, out),
        in_specs=[hbm] * 2,
        out_specs=(hbm, hbm),
        scratch_shapes=[vm(2, *cons.shape), dma((2, 5)), dma((2, 5))],
        name="hand_over",
    )(update, residual)

def solution(mesh):
    in_specs = (
        P(None, "stream", "span", None),
        P("stream", "span", None),
        P(None, None, "stream", "span", None),
    )
    out_specs = (P(None, "stream", "span", None), P(None, "stream", "span", None))
    return jax.shard_map(body, mesh=mesh, in_specs=in_specs, out_specs=out_specs, check_vma=False)
```
